32 devices in a mesh: ctx: 4 (over y, core), dp: 8 (over z, x).
Axes of the slice: x: 2, y: 2, z: 4, core: 2. Of those that a mesh axis runs over, the one named last changes fastest.
Arguments:
- x_tokens: bfloat16 [8, 512, 8192], P('dp', 'ctx'), may hold values from -6 to 6
- queries: bfloat16 [8, 512, 4096], P('dp', 'ctx'), may hold values from -110 to 110
- key_weight: bfloat16 [8192, 512], P('dp'), may hold values from -0.0625 to 0.0625
- value_weight: bfloat16 [8192, 512], P('dp'), may hold values from -0.0625 to 0.0625
- positions: int32 [8, 512], P('dp', 'ctx'), may hold values from 0 to 2097151, as said below
- block_lists: int32 [8, 8, 6], P('dp', 'ctx'), may hold values from 0 to 7, as said below
Outputs:
- attention_out: bfloat16 [8, 512, 4096], P('dp', 'ctx')
The draws below stay inside these ranges and needn't reach their ends.
Inputs may be any that keep to these rules, and one draw needn't show every extreme that they name: `block_lists`: entry i of row q of a sequence's lists is q - i when blocks q - i and q belong to the same document, else q; documents are runs of whole blocks, each of at most 6 blocks, and every sequence has one of exactly 6 blocks. `positions`: each sequence is four runs of 128 tokens; within a run the ids rise by one from token to token, and each run starts at or above the end of the run before it, so ids rise along the sequence.
All inputs are finite; a program needn't handle non-finite values.
Results may differ from the reference program's by a relative error of at most 0.007.
Values may be sent and summed in bfloat16 or wider, within the bound.
No kernel may reach another device: no remote copies, remote signals or barrier semaphores. Data moves between devices by JAX's collectives and lax.ppermute only.
A program may use at most 64 MiB of HBM per device.

```python
import math
import jax
import jax.numpy as jnp
from jax import lax

D = 8192
HD = 128
QH = 32
KVH = 4
TOK_DEV = 128
BLOCK = 64
SEQ = 512
BATCH = 8
NB = 8
MAXL = 6
QW = 4096
KVW = 512
N_CTX = 4


def draw_queries(key, part):
    first_key = jax.random.fold_in(key, 0)
    base_values = jnp.clip(jax.random.normal(first_key, (BATCH, SEQ, QW), jnp.float32), -4.0, 4.0)
    return base_values.astype(jnp.bfloat16)


def draw_positions(key, part):
    run_length = SEQ // 4
    skip_range = (2097152 - SEQ) // 4
    skip_key = jax.random.fold_in(key, 7)
    skips = jax.random.randint(skip_key, (BATCH, 4), 0, skip_range).astype(jnp.int32)
    row_ids = jnp.arange(BATCH, dtype=jnp.int32)[:, None]
    run_ids = jnp.arange(4, dtype=jnp.int32)[None, :]
    skips = jnp.where((row_ids == 0) & (run_ids == 0), 0, skips)
    starts = jnp.cumsum(skips, axis=1).astype(jnp.int32) + run_ids * run_length
    starts = jnp.where((row_ids == 0) & (run_ids == 3), 2097152 - run_length, starts)
    steps_in = jnp.arange(run_length, dtype=jnp.int32)[None, None, :]
    return (starts[:, :, None] + steps_in).reshape(BATCH, SEQ).astype(jnp.int32)


def draw_block_lists(key, part):
    cut_key, start_key = jax.random.split(key)
    block_ids = jnp.arange(NB, dtype=jnp.int32)[None, :]
    random_cuts = jax.random.randint(cut_key, (BATCH, NB), 0, 3) == 0
    long_start = jax.random.randint(start_key, (BATCH, 1), 0, NB - MAXL + 1)
    inside = (block_ids > long_start) & (block_ids < long_start + MAXL)
    boundaries = random_cuts & ~inside | (block_ids == long_start) | (block_ids == long_start + MAXL) | (block_ids == 0)
    documents = jnp.cumsum(boundaries.astype(jnp.int32), axis=1)
    offsets = jnp.arange(MAXL, dtype=jnp.int32)
    candidates = block_ids[:, :, None] - offsets[None, None, :]
    clipped = jnp.clip(candidates, 0, NB - 1)
    flat_index = jnp.broadcast_to(clipped.reshape(1, NB * MAXL), (BATCH, NB * MAXL))
    flat_docs = jnp.take_along_axis(documents, flat_index, axis=1)
    same_doc = (candidates >= 0) & (flat_docs.reshape(BATCH, NB, MAXL) == documents[:, :, None])
    return jnp.where(same_doc, candidates, block_ids[:, :, None]).astype(jnp.int32)


def shard_levels(rng, dims, cuts, smallest, largest):
    def one(dim, parts):
        draws = jax.random.uniform(jax.random.fold_in(jax.random.fold_in(rng, 6), dim), (parts,), jnp.float32, smallest / len(cuts), largest / len(cuts))
        return jnp.repeat(jnp.exp(draws), dims[dim] // parts).reshape((-1,) + (1,) * (len(dims) - dim - 1))

    factor_of = one(*cuts[0])
    for cut in cuts[1:]:
        factor_of = factor_of * one(*cut)
    return factor_of


def centred(key, extent, width, bound, shards=(), kind=jnp.bfloat16):
    values = width * jax.random.normal(key, extent, jnp.float32)
    if shards:
        values = values * shard_levels(key, extent, shards, -0.22, 0.18)
    return jnp.clip(values, -bound, bound).astype(kind)


def setup_inputs(seed: int = 0) -> dict:
    arg_keys = jax.random.split(jax.random.key(seed), 7)
    return {
        "x_tokens": centred(arg_keys[0], (BATCH, SEQ, D), 1.0, 6.0, ((0, 8), (1, 4))),
        "queries": draw_queries(jax.random.fold_in(arg_keys[6], 71), 0),
        "key_weight": centred(arg_keys[2], (D, KVW), D ** -0.5, 0.0625, ((0, 8),)),
        "value_weight": centred(arg_keys[3], (D, KVW), D ** -0.5, 0.0625, ((0, 8),)),
        "positions": draw_positions(jax.random.fold_in(arg_keys[6], 71), 0),
        "block_lists": draw_block_lists(jax.random.fold_in(arg_keys[6], 71), 0),
    }


neg_large = -1.0e30


def rope_periods(half_width):
    return jnp.array([int(2.0 * math.pi * 500000.0 ** (column / half_width) + 0.5) for column in range(half_width)], jnp.int32)


def rotate_pairs(features, token_pos, head_size):
    half_width = head_size // 2
    periods = rope_periods(half_width)
    turn_counts = jnp.remainder(token_pos[:, None], periods[None, :])
    angles = (2.0 * math.pi) * turn_counts.astype(jnp.float32) / periods.astype(jnp.float32)
    cosine = jnp.cos(angles)[:, None, :]
    sine_part = jnp.sin(angles)[:, None, :]
    shaped = features.reshape(features.shape[0], -1, head_size)
    first_half = shaped[:, :, :half_width]
    second_half = shaped[:, :, half_width:]
    turned = jnp.concatenate([first_half * cosine - second_half * sine_part, second_half * cosine + first_half * sine_part], axis=2)
    return turned.reshape(features.shape[0], -1)


def reference(x_tokens, queries, key_weight, value_weight, positions, block_lists):
    scale_factor = HD ** -0.5
    group_size = QH // KVH

    def one_sequence(inputs):
        tokens_in, query_in, token_pos, lists_in = inputs
        key_proj = jnp.dot(tokens_in, key_weight, preferred_element_type=jnp.float32)
        value_proj = jnp.dot(tokens_in, value_weight, preferred_element_type=jnp.float32)
        key_rot = rotate_pairs(key_proj, token_pos, HD).astype(jnp.bfloat16)
        value_cast = value_proj.astype(jnp.bfloat16)
        query_rot = rotate_pairs(query_in.astype(jnp.float32), token_pos, HD).astype(jnp.bfloat16)
        member = jnp.any(lists_in[:, :, None] == jnp.arange(NB, dtype=jnp.int32)[None, None, :], axis=1)
        key_index = jnp.arange(SEQ, dtype=jnp.int32)
        key_blocks = key_index // BLOCK
        keys_float = lax.optimization_barrier(key_rot).astype(jnp.float32).reshape(SEQ, KVH, HD)
        values_float = lax.optimization_barrier(value_cast).astype(jnp.float32).reshape(SEQ, KVH, HD)
        query_shards = lax.optimization_barrier(query_rot).reshape(N_CTX, TOK_DEV, KVH, group_size, HD)

        def one_shard(shard_inputs):
            shard_number, query_block = shard_inputs
            query_index = shard_number * TOK_DEV + jnp.arange(TOK_DEV, dtype=jnp.int32)
            block_rows = member[query_index // BLOCK]
            allowed = block_rows[:, key_blocks] & (key_index[None, :] <= query_index[:, None])
            scores = jnp.einsum("tkgd,skd->kgts", query_block.astype(jnp.float32), keys_float) * scale_factor
            masked = jnp.where(allowed, scores, neg_large)
            row_top = jnp.max(masked, axis=3, keepdims=True)
            probabilities = jnp.where(allowed, jnp.exp(scores - row_top), 0.0)
            row_total = jnp.sum(probabilities, axis=3)
            soft_weights = lax.optimization_barrier(probabilities.astype(jnp.bfloat16)).astype(jnp.float32)
            summed = jnp.einsum("kgts,skd->tkgd", soft_weights, values_float)
            mixed = summed / jnp.transpose(row_total, (2, 0, 1))[:, :, :, None]
            return mixed.reshape(TOK_DEV, QW).astype(jnp.bfloat16)

        shard_ids = jnp.arange(N_CTX, dtype=jnp.int32)
        outputs = lax.map(one_shard, (shard_ids, query_shards))
        return outputs.reshape(SEQ, QW)

    return lax.map(one_sequence, (x_tokens, queries, positions, block_lists))
```

```python
import functools
import math

import jax
import jax.numpy as jnp
from jax import lax
from jax.experimental import pallas as pl
from jax.experimental.pallas import tpu as pltpu
from jax.sharding import PartitionSpec as P

HD = 128
BLOCK = 64
LOG2E = 1.4426950408889634

neg_large = -1e30
ANY = pl.BlockSpec(memory_space=pl.ANY)
VMEM = pl.BlockSpec(memory_space=pltpu.VMEM)
SMEM = pl.BlockSpec(memory_space=pltpu.SMEM)
PARAMS = pltpu.CompilerParams(vmem_limit_bytes=40 * 1024 * 1024)


def cost(flops, bytes_accessed, transcendentals=0):
    return pl.CostEstimate(
        flops=flops, bytes_accessed=bytes_accessed, transcendentals=transcendentals
    )


def rope_periods(half_width):
    return jnp.array(
        [
            int(2.0 * math.pi * 500000.0 ** (column / half_width) + 0.5)
            for column in range(half_width)
        ],
        jnp.int32,
    )


def rope_tables(token_pos):
    half_width = HD // 2
    periods = rope_periods(half_width)
    turn_counts = jnp.remainder(token_pos[:, None], periods[None, :])
    angles = 2.0 * math.pi * turn_counts.astype(jnp.float32) / periods.astype(jnp.float32)
    cosine = jnp.cos(angles)
    sine_part = jnp.sin(angles)
    return (
        jnp.concatenate([cosine, cosine], axis=1),
        jnp.concatenate([-sine_part, sine_part], axis=1),
    )


def turn(head, cosine, sine_part):
    return head * cosine + pltpu.roll(head, HD // 2, 1) * sine_part


def cut_weights_kernel(where, key_ref, value_ref, key_out, value_out, sems):
    rows, columns = key_out.shape
    y, core = where[2], where[3]
    copies = []
    for i, (src, dst) in enumerate(((key_ref, key_out), (value_ref, value_out))):
        copy = pltpu.make_async_copy(
            src.at[
                pl.ds(pl.multiple_of(y * rows, rows), rows),
                pl.ds(pl.multiple_of(core * columns, columns), columns),
            ],
            dst,
            sems.at[i],
        )
        copy.start()
        copies.append(copy)
    for copy in copies:
        copy.wait()


def cut_tokens_kernel(n_line, where, x_ref, mine_ref, other_ref, sems):
    z, x, y = where[0], where[1], where[2]
    width = mine_ref.shape[2]
    copies = []
    for side, dst in ((0, other_ref), (1, mine_ref)):
        for j in range(n_line):
            shard = lax.rem(z - j + n_line, n_line) * 2 + (x if side else 1 - x)
            for h in range(2):
                half = 1 - y if h else y
                start = pl.multiple_of((shard * 2 + half) * width, width)
                copy = pltpu.make_async_copy(
                    x_ref.at[:, pl.ds(start, width)],
                    dst.at[2 * j + h],
                    sems.at[side, 2 * j + h],
                )
                copy.start()
                copies.append(copy)
    for copy in copies:
        copy.wait()


def project_kernel(n_parts, where, *refs):
    x_refs, own_ref = refs[:4], refs[4]
    piece_refs = refs[5 : 5 + n_parts - 2]
    own_out, other_out, x_buf, w_buf, x_sems, w_sems = refs[5 + n_parts - 2 :]
    y, core = where[2], where[3]
    tokens = x_refs[0].shape[1]
    rows, columns = w_buf.shape[1:]
    places = (core, 1 - core, 2 + core, 3 - core)
    copies = []
    for p in range(n_parts):
        if p < 2:
            half = y if p == 0 else 1 - y
            src = own_ref.at[
                pl.ds(pl.multiple_of(half * rows, rows), rows),
                pl.ds(pl.multiple_of(core * columns, columns), columns),
            ]
        else:
            src = piece_refs[p - 2]
        copies.append([pltpu.make_async_copy(src, w_buf.at[p], w_sems.at[p])])
        for a in range(4):
            copies[p].append(
                pltpu.make_async_copy(
                    x_refs[a].at[p],
                    x_buf.at[p, pl.ds(pl.multiple_of(places[a] * tokens, tokens), tokens), :],
                    x_sems.at[p, a],
                )
            )
        for copy in copies[p]:
            copy.start()
    total = None
    for p in range(n_parts):
        for copy in copies[p]:
            copy.wait()
        term = jnp.dot(x_buf[p], w_buf[p], preferred_element_type=jnp.float32)
        total = term if total is None else total + term
    own_out[...] = total[: 2 * tokens]
    other_out[...] = total[2 * tokens :].astype(other_out.dtype)


def project(where, x_parts, own_weight, pieces, other_dtype):
    n_parts, tokens, rows = x_parts[0].shape
    columns = own_weight.shape[1] // 2
    return pl.pallas_call(
        functools.partial(project_kernel, n_parts),
        out_shape=(
            jax.ShapeDtypeStruct((2 * tokens, columns), jnp.float32),
            jax.ShapeDtypeStruct((2 * tokens, columns), other_dtype),
        ),
        in_specs=[SMEM] + [ANY] * (5 + len(pieces)),
        out_specs=(VMEM, VMEM),
        scratch_shapes=[
            pltpu.VMEM((n_parts, 4 * tokens, rows), jnp.bfloat16),
            pltpu.VMEM((n_parts, rows, columns), jnp.bfloat16),
            pltpu.SemaphoreType.DMA((n_parts, 4)),
            pltpu.SemaphoreType.DMA((n_parts,)),
        ],
        compiler_params=PARAMS,
        cost_estimate=cost(
            2 * 4 * tokens * n_parts * rows * columns,
            2 * n_parts * rows * (4 * tokens + columns) + 16 * tokens * columns,
        ),
    )(where, *x_parts, own_weight, *pieces)


def finish_keys_kernel(own_ref, came_ref, cosine_ref, sine_ref, out_ref):
    for h in range(out_ref.shape[1] // HD):
        span = slice(h * HD, (h + 1) * HD)
        key = own_ref[:, span] + came_ref[:, span]
        out_ref[:, span] = turn(key, cosine_ref[...], sine_ref[...]).astype(jnp.bfloat16)


def turn_queries_kernel(q_ref, cosine_ref, sine_ref, out_ref):
    for h in range(out_ref.shape[0]):
        query = q_ref[:, h * HD : (h + 1) * HD].astype(jnp.float32)
        out_ref[h] = turn(query, cosine_ref[...], sine_ref[...]).astype(jnp.bfloat16)


def attend_kernel(n_chips, group, where, q_ref, bias_ref, *refs):
    key_refs, value_refs, out_ref = refs[:2], refs[2:4], refs[4]
    core = where[3]
    heads_here = key_refs[0].shape[2] // HD
    span_rows = key_refs[0].shape[1]
    bias = bias_ref[...]
    scale = HD ** (-0.5) * LOG2E
    for side in range(2):
        first_head = (1 - core if side else core) * heads_here
        for i in range(heads_here):
            span = slice(i * HD, (i + 1) * HD)
            keys = key_refs[side][:, :, span].reshape(n_chips * span_rows, HD)
            values = value_refs[side][:, :, span].reshape(n_chips * span_rows, HD)
            for g in range(group):
                head = (first_head + i) * group + g
                query = q_ref[head]
                scores = lax.dot_general(
                    query, keys, (((1,), (1,)), ((), ())), preferred_element_type=jnp.float32
                )
                scores = scores + bias
                top = jnp.max(scores, axis=1, keepdims=True)
                probabilities = jnp.exp2((scores - top) * scale)
                row_total = jnp.sum(probabilities, axis=1, keepdims=True)
                mixed = jnp.dot(
                    probabilities.astype(jnp.bfloat16),
                    values,
                    preferred_element_type=jnp.float32,
                )
                out_ref[:, pl.ds(pl.multiple_of(head * HD, HD), HD)] = (
                    mixed / row_total
                ).astype(jnp.bfloat16)


def on_device(n_ctx, n_dp, x_tokens, queries, key_weight, value_weight, positions, block_lists):
    n_line, n_chips = n_dp // 2, n_ctx // 2
    tokens_local, query_local = x_tokens[0], queries[0]
    tok_rows, query_width = query_local.shape
    shard_rows, key_width = key_weight.shape
    half_rows, half_columns = shard_rows // 2, key_width // 2
    group = query_width // key_width
    ctx, dp = lax.axis_index("ctx"), lax.axis_index("dp")
    chip, core = ctx // 2, ctx % 2
    y = chip % 2
    where = jnp.stack([dp // 2, dp % 2, y, core]).astype(jnp.int32)

    def over_core(array):
        return lax.ppermute(array, "ctx", [(i, i ^ 1) for i in range(n_ctx)])

    def over_y(array):
        return lax.ppermute(array, "ctx", [(i, i ^ 2) for i in range(n_ctx)])

    def over_x(array):
        return lax.ppermute(array, "dp", [(i, i ^ 1) for i in range(n_dp)])

    def over_z(array, step):
        return lax.ppermute(array, "dp", [(i, (i + 2 * step) % n_dp) for i in range(n_dp)])

    def from_chip(array, step, across_x=False):
        if not across_x:
            return lax.ppermute(
                array, "ctx", [(i, (i + 2 * step) % n_ctx) for i in range(n_ctx)]
            )
        pairs = [
            (i * n_dp + d, ((i + 2 * step) % n_ctx) * n_dp + (d ^ 1))
            for i in range(n_ctx)
            for d in range(n_dp)
        ]
        return lax.ppermute(array, ("ctx", "dp"), pairs)

    key_own, value_own = pl.pallas_call(
        cut_weights_kernel,
        out_shape=(jax.ShapeDtypeStruct((half_rows, half_columns), jnp.bfloat16),) * 2,
        in_specs=[SMEM, ANY, ANY],
        out_specs=(ANY, ANY),
        scratch_shapes=[pltpu.SemaphoreType.DMA((2,))],
        cost_estimate=cost(0, 8 * half_rows * half_columns),
    )(where, key_weight, value_weight)
    mine, other = pl.pallas_call(
        functools.partial(cut_tokens_kernel, n_line),
        out_shape=(jax.ShapeDtypeStruct((2 * n_line, tok_rows, half_rows), jnp.bfloat16),) * 2,
        in_specs=[SMEM, ANY],
        out_specs=(ANY, ANY),
        scratch_shapes=[pltpu.SemaphoreType.DMA((2, 2 * n_line))],
        cost_estimate=cost(0, 4 * tokens_local.size),
    )(where, tokens_local)

    def gather_pieces(own):
        came = [None] * n_line
        up = n_line // 2
        came[0] = own
        for j in range(1, up + 1):
            came[j] = over_z(came[j - 1], 1)
            k = n_line - j
            if k > up:
                came[k] = over_z(came[(k + 1) % n_line], -1)
        pieces = []
        for j in range(1, n_line):
            pieces += [came[j], over_y(came[j])]
        return pieces

    key_pieces = gather_pieces(key_own)
    neighbour = over_x(other)
    value_pieces = gather_pieces(value_own)
    sibling = over_core(mine)
    neighbour_sibling = over_core(neighbour)
    x_parts = (mine, sibling, neighbour, neighbour_sibling)

    token_pos = positions[0]
    pos_pair = jnp.stack([token_pos, over_core(positions)[0]])
    pos_chip = jnp.where(core == 0, pos_pair, pos_pair[::-1]).reshape(-1)
    cosine, sine_part = rope_tables(pos_chip)
    own_rows = core * tok_rows
    query_cosine = lax.dynamic_slice_in_dim(cosine, own_rows, tok_rows, 0)
    query_sine = lax.dynamic_slice_in_dim(sine_part, own_rows, tok_rows, 0)
    n_heads = query_width // HD
    query_rot = pl.pallas_call(
        turn_queries_kernel,
        out_shape=jax.ShapeDtypeStruct((n_heads, tok_rows, HD), jnp.bfloat16),
        in_specs=[VMEM] * 3,
        out_specs=VMEM,
        cost_estimate=cost(3 * query_local.size, 4 * query_local.size),
    )(query_local, query_cosine, query_sine)

    chip_rows = 2 * tok_rows
    source_chip = jnp.remainder(chip - jnp.arange(n_chips, dtype=jnp.int32), n_chips)
    key_index = (
        source_chip[:, None] * chip_rows + jnp.arange(chip_rows, dtype=jnp.int32)[None, :]
    ).reshape(-1)
    query_index = ctx * tok_rows + jnp.arange(tok_rows, dtype=jnp.int32)
    member = jnp.any(
        block_lists[0][:, :, None] == (key_index // BLOCK)[None, None, :], axis=1
    )
    allowed = jnp.repeat(member, BLOCK, axis=0) & (key_index[None, :] <= query_index[:, None])
    bias = jnp.where(allowed, 0.0, neg_large).astype(jnp.float32)

    key_part, key_away = project(where, x_parts, key_weight, key_pieces, jnp.float32)
    key_here = pl.pallas_call(
        finish_keys_kernel,
        out_shape=jax.ShapeDtypeStruct(key_part.shape, jnp.bfloat16),
        in_specs=[VMEM] * 4,
        out_specs=VMEM,
        cost_estimate=cost(4 * key_part.size, 10 * key_part.size),
    )(key_part, over_x(key_away), cosine, sine_part)
    keys = jnp.stack([key_here] + [from_chip(key_here, j) for j in range(1, n_chips)])
    keys_other = over_core(keys)

    value_part, value_away = project(where, x_parts, value_weight, value_pieces, jnp.bfloat16)
    value_sent = value_part.astype(jnp.bfloat16)
    value_list = [value_part + over_x(value_away).astype(jnp.float32)]
    for j in range(1, n_chips):
        value_list.append(
            from_chip(value_sent, j).astype(jnp.float32)
            + from_chip(value_away, j, True).astype(jnp.float32)
        )
    values = jnp.stack(value_list).astype(jnp.bfloat16)
    values_other = over_core(values)

    span_rows = n_chips * chip_rows
    mixed = pl.pallas_call(
        functools.partial(attend_kernel, n_chips, group),
        out_shape=jax.ShapeDtypeStruct((tok_rows, query_width), jnp.bfloat16),
        in_specs=[SMEM] + [VMEM] * 6,
        out_specs=VMEM,
        compiler_params=PARAMS,
        cost_estimate=cost(
            4 * tok_rows * query_width * span_rows,
            4 * (tok_rows * query_width + span_rows * key_width),
            tok_rows * n_heads * span_rows,
        ),
    )(where, query_rot, bias, keys, keys_other, values, values_other)
    return mixed[None]


def solution(mesh):
    return jax.shard_map(
        functools.partial(on_device, mesh.shape["ctx"], mesh.shape["dp"]),
        mesh=mesh,
        in_specs=(
            P("dp", "ctx", None),
            P("dp", "ctx", None),
            P("dp", None),
            P("dp", None),
            P("dp", "ctx"),
            P("dp", "ctx", None),
        ),
        out_specs=P("dp", "ctx", None),
        check_vma=False,
    )
```

```python
import functools
import math

import jax
import jax.numpy as jnp
from jax import lax
from jax.experimental import pallas as pl
from jax.experimental.pallas import tpu as pltpu
from jax.sharding import PartitionSpec as P

HD = 128
BLOCK = 64
LOG2E = 1.4426950408889634

neg_large = -1e30
ANY = pl.BlockSpec(memory_space=pl.ANY)
VMEM = pl.BlockSpec(memory_space=pltpu.VMEM)
SMEM = pl.BlockSpec(memory_space=pltpu.SMEM)


def params(held):
    return pltpu.CompilerParams(vmem_limit_bytes=held + 6 * 1024 * 1024)


def cost(flops, bytes_accessed, transcendentals=0):
    return pl.CostEstimate(
        flops=flops, bytes_accessed=bytes_accessed, transcendentals=transcendentals
    )


def rope_periods(half_width):
    return jnp.array(
        [
            int(2.0 * math.pi * 500000.0 ** (column / half_width) + 0.5)
            for column in range(half_width)
        ],
        jnp.int32,
    )


def rope_tables(token_pos):
    half_width = HD // 2
    periods = rope_periods(half_width)
    turn_counts = jnp.remainder(token_pos[:, None], periods[None, :])
    angles = 2.0 * math.pi * turn_counts.astype(jnp.float32) / periods.astype(jnp.float32)
    cosine = jnp.cos(angles)
    sine_part = jnp.sin(angles)
    return (
        jnp.concatenate([cosine, cosine], axis=1),
        jnp.concatenate([-sine_part, sine_part], axis=1),
    )


def turn(head, cosine, sine_part):
    return head * cosine + pltpu.roll(head, HD // 2, 1) * sine_part


def cut_weight_kernel(where, weight_ref, *refs):
    out_ref, sem = refs[-2:]
    rows, columns = out_ref.shape
    y, core = where[2], where[3]
    copy = pltpu.make_async_copy(
        weight_ref.at[
            pl.ds(pl.multiple_of(y * rows, rows), rows),
            pl.ds(pl.multiple_of(core * columns, columns), columns),
        ],
        out_ref,
        sem,
    )
    copy.start()
    copy.wait()


def cut_weight(where, weight, *after):
    rows, columns = weight.shape[0] // 2, weight.shape[1] // 2
    return pl.pallas_call(
        cut_weight_kernel,
        out_shape=jax.ShapeDtypeStruct((rows, columns), jnp.bfloat16),
        in_specs=[SMEM, ANY] + [ANY] * len(after),
        out_specs=VMEM,
        scratch_shapes=[pltpu.SemaphoreType.DMA(())],
        compiler_params=params(2 * rows * columns),
        cost_estimate=cost(0, 4 * rows * columns),
    )(where, weight, *after)


def cut_tokens_kernel(n_line, where, x_ref, *refs):
    out_refs, sems = refs[-5:-1], refs[-1]
    z, x, y = where[0], where[1], where[2]
    width = out_refs[0].shape[2]
    copies = []
    for i in (1, 2, 3, 0):
        for j in range(n_line):
            shard = lax.rem(z - j + n_line, n_line) * 2 + (1 - x if i & 1 else x)
            half = 1 - y if i & 2 else y
            start = pl.multiple_of((shard * 2 + half) * width, width)
            copy = pltpu.make_async_copy(
                x_ref.at[:, pl.ds(start, width)], out_refs[i].at[j], sems.at[i, j]
            )
            copy.start()
            copies.append(copy)
    for copy in copies:
        copy.wait()


def cut_tokens(where, tokens, n_line, *after):
    rows, columns = tokens.shape
    width = columns // (4 * n_line)
    return pl.pallas_call(
        functools.partial(cut_tokens_kernel, n_line),
        out_shape=(jax.ShapeDtypeStruct((n_line, rows, width), jnp.bfloat16),) * 4,
        in_specs=[SMEM, ANY] + [ANY] * len(after),
        out_specs=(VMEM,) * 4,
        scratch_shapes=[pltpu.SemaphoreType.DMA((4, n_line))],
        compiler_params=params(2 * tokens.size),
        cost_estimate=cost(0, 4 * tokens.size),
    )(where, tokens, *after)


def project_kernel(n_sets, n_parts, with_start, n_after, where, *refs):
    refs = list(refs)
    x_refs, refs = refs[: 2 * n_sets], refs[2 * n_sets :]
    w_refs, refs = refs[:n_parts], refs[n_parts:]
    start_refs, refs = (refs[:n_sets], refs[n_sets:]) if with_start else (None, refs)
    outs = refs[n_after:]
    core = where[3]
    tokens = x_refs[0].shape[1]
    for s in range(n_sets):
        for side in range(2):
            x_ref = x_refs[2 * s + side]
            place = pl.ds(pl.multiple_of((1 - core if side else core) * tokens, tokens), tokens)
            total = start_refs[s][place, :] if with_start else None
            for j in range(n_parts):
                term = jnp.dot(x_ref[j], w_refs[j][...], preferred_element_type=jnp.float32)
                total = term if total is None else total + term
            for out in outs[s::n_sets]:
                out[place, :] = total.astype(out.dtype)


def project(where, sets, first, pieces, starts, out_types, *after):
    n_line, tokens, rows = sets[0][0].shape
    columns = pieces[0].shape[1]
    n_parts, n_sets = len(pieces), len(sets)
    blocks = first // n_parts
    x_spec = pl.BlockSpec((n_parts, tokens, rows), lambda: (blocks, 0, 0))
    x_args = [array for pair in sets for array in pair]
    starts = list(starts or [])
    shapes = tuple(
        jax.ShapeDtypeStruct((2 * tokens, columns), t) for t in out_types for _ in sets
    )
    held = n_sets * 4 * tokens * (n_parts * rows + 4 * columns) + 2 * n_parts * rows * columns
    return pl.pallas_call(
        functools.partial(project_kernel, n_sets, n_parts, bool(starts), len(after)),
        out_shape=shapes,
        in_specs=[SMEM]
        + [x_spec] * len(x_args)
        + [VMEM] * (n_parts + len(starts))
        + [ANY] * len(after),
        out_specs=(VMEM,) * len(shapes),
        compiler_params=params(held),
        cost_estimate=cost(4 * n_sets * tokens * n_parts * rows * columns, held),
    )(where, *x_args, *pieces, *starts, *after)


def add_up(refs, span=slice(None)):
    total = refs[0][:, span].astype(jnp.float32)
    for ref in refs[1:]:
        total = total + ref[:, span].astype(jnp.float32)
    return total


def finish_keys_kernel(own_ref, x_ref, y_ref, xy_ref, cosine_ref, sine_ref, out_ref):
    for h in range(out_ref.shape[1] // HD):
        span = slice(h * HD, (h + 1) * HD)
        key = add_up((own_ref, x_ref, y_ref, xy_ref), span)
        out_ref[:, span] = turn(key, cosine_ref[...], sine_ref[...]).astype(jnp.bfloat16)


def finish_values_kernel(own_ref, x_ref, y_ref, xy_ref, out_ref):
    out_ref[...] = add_up((own_ref, x_ref, y_ref, xy_ref)).astype(jnp.bfloat16)


def turn_queries_kernel(q_ref, cosine_ref, sine_ref, after_ref, out_ref):
    for h in range(out_ref.shape[0]):
        query = q_ref[:, h * HD : (h + 1) * HD].astype(jnp.float32)
        out_ref[h] = turn(query, cosine_ref[...], sine_ref[...]).astype(jnp.bfloat16)


def weigh_kernel(n_chips, group, where, q_ref, bias_ref, *refs):
    key_refs, weight_ref, total_ref = refs[: 2 * n_chips], refs[-2], refs[-1]
    core = where[3]
    heads_here = key_refs[0].shape[1] // HD
    bias = bias_ref[...]
    scale = HD ** (-0.5) * LOG2E
    lane = lax.broadcasted_iota(jnp.int32, total_ref.shape, 1)
    totals = jnp.zeros(total_ref.shape, jnp.float32)
    for side in range(2):
        first_head = (1 - core if side else core) * heads_here
        for i in range(heads_here):
            span = slice(i * HD, (i + 1) * HD)
            keys = jnp.concatenate(
                [ref[:, span] for ref in key_refs[side * n_chips : (side + 1) * n_chips]], axis=0
            )
            for g in range(group):
                slot = (side * heads_here + i) * group + g
                query = q_ref[(first_head + i) * group + g]
                scores = lax.dot_general(
                    query, keys, (((1,), (1,)), ((), ())), preferred_element_type=jnp.float32
                )
                scores = scores + bias
                top = jnp.max(scores, axis=1, keepdims=True)
                probabilities = jnp.exp2((scores - top) * scale)
                row_total = jnp.sum(probabilities, axis=1, keepdims=True)
                totals = jnp.where(lane == slot, row_total, totals)
                weight_ref[slot] = probabilities.astype(jnp.bfloat16)
    total_ref[...] = totals


def mix_kernel(n_chips, group, where, weight_ref, total_ref, *refs):
    value_refs, out_ref = refs[: 2 * n_chips], refs[-1]
    core = where[3]
    heads_here = value_refs[0].shape[1] // HD
    tokens, span_rows = weight_ref.shape[1:]
    inverse = 1.0 / total_ref[...]
    for side in range(2):
        first_head = (1 - core if side else core) * heads_here
        for i in range(heads_here):
            span = slice(i * HD, (i + 1) * HD)
            values = jnp.concatenate(
                [ref[:, span] for ref in value_refs[side * n_chips : (side + 1) * n_chips]],
                axis=0,
            )
            slot = (side * heads_here + i) * group
            mixed = jnp.dot(
                weight_ref[slot : slot + group].reshape(group * tokens, span_rows),
                values,
                preferred_element_type=jnp.float32,
            )
            for g in range(group):
                head = (first_head + i) * group + g
                out_ref[:, pl.ds(pl.multiple_of(head * HD, HD), HD)] = (
                    mixed[g * tokens : (g + 1) * tokens] * inverse[:, slot + g : slot + g + 1]
                ).astype(jnp.bfloat16)


def on_device(n_ctx, n_dp, x_tokens, queries, key_weight, value_weight, positions, block_lists):
    n_line, n_chips = n_dp // 2, n_ctx // 2
    tokens_local, query_local = x_tokens[0], queries[0]
    tok_rows, query_width = query_local.shape
    shard_rows, key_width = key_weight.shape
    half_rows, half_columns = shard_rows // 2, key_width // 2
    group = query_width // key_width
    ctx, dp = lax.axis_index("ctx"), lax.axis_index("dp")
    chip, core = ctx // 2, ctx % 2
    y = chip % 2
    where = jnp.stack([dp // 2, dp % 2, y, core]).astype(jnp.int32)

    def over_core(array):
        return lax.ppermute(array, "ctx", [(i, i ^ 1) for i in range(n_ctx)])

    def over_y(array):
        return lax.ppermute(array, "ctx", [(i, i ^ 2) for i in range(n_ctx)])

    def over_x(array):
        return lax.ppermute(array, "dp", [(i, i ^ 1) for i in range(n_dp)])

    def over_z(array, step):
        return lax.ppermute(array, "dp", [(i, (i + 2 * step) % n_dp) for i in range(n_dp)])

    def over_xy(array):
        pairs = [
            (i * n_dp + d, (i ^ 2) * n_dp + (d ^ 1)) for i in range(n_ctx) for d in range(n_dp)
        ]
        return lax.ppermute(array, ("ctx", "dp"), pairs)

    def from_chip(array, step):
        return lax.ppermute(array, "ctx", [(i, (i + 2 * step) % n_ctx) for i in range(n_ctx)])

    up = n_line // 2

    def gather_pieces(own):
        came = [None] * n_line
        came[0] = own
        for j in range(1, up + 1):
            came[j] = over_z(came[j - 1], 1)
            k = n_line - j
            if k > up:
                came[k] = over_z(came[(k + 1) % n_line], -1)
        return came

    key_own = cut_weight(where, key_weight)
    key_pieces = gather_pieces(key_own)
    cuts = cut_tokens(where, tokens_local, n_line, key_own)
    held = [cuts[0], over_x(cuts[1]), over_y(cuts[2]), over_xy(cuts[3])]
    value_own = cut_weight(where, value_weight, key_pieces[1], cuts[0])
    value_pieces = gather_pieces(value_own)
    sets = [(array, over_core(array)) for array in held]

    token_pos = positions[0]
    pos_pair = jnp.stack([token_pos, over_core(positions)[0]])
    pos_chip = jnp.where(core == 0, pos_pair, pos_pair[::-1]).reshape(-1)
    cosine, sine_part = rope_tables(pos_chip)
    own_rows = core * tok_rows
    query_cosine = lax.dynamic_slice_in_dim(cosine, own_rows, tok_rows, 0)
    query_sine = lax.dynamic_slice_in_dim(sine_part, own_rows, tok_rows, 0)
    n_heads = query_width // HD
    query_rot = pl.pallas_call(
        turn_queries_kernel,
        out_shape=jax.ShapeDtypeStruct((n_heads, tok_rows, HD), jnp.bfloat16),
        in_specs=[VMEM] * 3 + [ANY],
        out_specs=VMEM,
        compiler_params=params(4 * query_local.size),
        cost_estimate=cost(3 * query_local.size, 4 * query_local.size),
    )(query_local, query_cosine, query_sine, cuts[0])

    chip_rows = 2 * tok_rows
    source_chip = jnp.remainder(chip - jnp.arange(n_chips, dtype=jnp.int32), n_chips)
    key_index = (
        source_chip[:, None] * chip_rows + jnp.arange(chip_rows, dtype=jnp.int32)[None, :]
    ).reshape(-1)
    query_index = ctx * tok_rows + jnp.arange(tok_rows, dtype=jnp.int32)
    member = jnp.any(
        block_lists[0][:, :, None] == (key_index // BLOCK)[None, None, :], axis=1
    )
    allowed = jnp.repeat(member, BLOCK, axis=0) & (key_index[None, :] <= query_index[:, None])
    bias = jnp.where(allowed, 0.0, neg_large).astype(jnp.float32)

    f32, bf16 = jnp.float32, jnp.bfloat16
    key_parts = project(
        where, sets, 0, key_pieces, None, (f32,), query_rot, bias, cosine, sine_part
    )
    key_here = pl.pallas_call(
        finish_keys_kernel,
        out_shape=jax.ShapeDtypeStruct(key_parts[0].shape, bf16),
        in_specs=[VMEM] * 6,
        out_specs=VMEM,
        compiler_params=params(26 * key_parts[0].size),
        cost_estimate=cost(6 * key_parts[0].size, 26 * key_parts[0].size),
    )(
        key_parts[0], over_x(key_parts[1]), over_y(key_parts[2]), over_xy(key_parts[3]),
        cosine, sine_part,
    )
    keys = [key_here] + [from_chip(key_here, j) for j in range(1, n_chips)]
    keys += [over_core(array) for array in keys]

    value_parts = project(where, sets, 0, value_pieces, None, (bf16,), key_parts[0])
    value_here = pl.pallas_call(
        finish_values_kernel,
        out_shape=jax.ShapeDtypeStruct(value_parts[0].shape, bf16),
        in_specs=[VMEM] * 4,
        out_specs=VMEM,
        compiler_params=params(10 * value_parts[0].size),
        cost_estimate=cost(3 * value_parts[0].size, 10 * value_parts[0].size),
    )(value_parts[0], over_x(value_parts[1]), over_y(value_parts[2]), over_xy(value_parts[3]))
    values = [value_here] + [from_chip(value_here, j) for j in range(1, n_chips)]
    values += [over_core(array) for array in values]

    span_rows = n_chips * chip_rows
    weights, totals = pl.pallas_call(
        functools.partial(weigh_kernel, n_chips, group),
        out_shape=(
            jax.ShapeDtypeStruct((n_heads, tok_rows, span_rows), bf16),
            jax.ShapeDtypeStruct((tok_rows, HD), f32),
        ),
        in_specs=[SMEM] + [VMEM] * (2 + len(keys)),
        out_specs=(VMEM, VMEM),
        compiler_params=params(
            tok_rows * (4 * query_width + 2 * n_heads * span_rows + 8 * span_rows)
        ),
        cost_estimate=cost(
            2 * tok_rows * query_width * span_rows,
            2 * tok_rows * (query_width + n_heads * span_rows),
            tok_rows * n_heads * span_rows,
        ),
    )(where, query_rot, bias, *keys)
    mixed = pl.pallas_call(
        functools.partial(mix_kernel, n_chips, group),
        out_shape=jax.ShapeDtypeStruct((tok_rows, query_width), bf16),
        in_specs=[SMEM] + [VMEM] * (2 + len(values)),
        out_specs=VMEM,
        compiler_params=params(
            tok_rows * (4 * query_width + 2 * n_heads * span_rows) + 4 * span_rows * key_width
        ),
        cost_estimate=cost(
            2 * tok_rows * query_width * span_rows,
            2 * tok_rows * (query_width + n_heads * span_rows),
        ),
    )(where, weights, totals, *values)
    return mixed[None]


def solution(mesh):
    return jax.shard_map(
        functools.partial(on_device, mesh.shape["ctx"], mesh.shape["dp"]),
        mesh=mesh,
        in_specs=(
            P("dp", "ctx", None),
            P("dp", "ctx", None),
            P("dp", None),
            P("dp", None),
            P("dp", "ctx"),
            P("dp", "ctx", None),
        ),
        out_specs=P("dp", "ctx", None),
        check_vma=False,
    )
```

```python
import functools
import math

import jax
import jax.numpy as jnp
from jax import lax
from jax.experimental import pallas as pl
from jax.experimental.pallas import tpu as pltpu
from jax.sharding import PartitionSpec as P

HD = 128
BLOCK = 64
LOG2E = 1.4426950408889634

neg_large = -1e30
HEADROOM = 2 * 1024 * 1024
ANY = pl.BlockSpec(memory_space=pl.ANY)
VMEM = pl.BlockSpec(memory_space=pltpu.VMEM)
SMEM = pl.BlockSpec(memory_space=pltpu.SMEM)


def params(held):
    return pltpu.CompilerParams(vmem_limit_bytes=held + HEADROOM)


def cost(flops, bytes_accessed, transcendentals=0):
    return pl.CostEstimate(
        flops=flops, bytes_accessed=bytes_accessed, transcendentals=transcendentals
    )


def rope_periods(half_width):
    return jnp.array(
        [
            int(2.0 * math.pi * 500000.0 ** (column / half_width) + 0.5)
            for column in range(half_width)
        ],
        jnp.int32,
    )


def rope_tables(token_pos):
    half_width = HD // 2
    periods = rope_periods(half_width)
    turn_counts = jnp.remainder(token_pos[:, None], periods[None, :])
    angles = 2.0 * math.pi * turn_counts.astype(jnp.float32) / periods.astype(jnp.float32)
    cosine = jnp.cos(angles)
    sine_part = jnp.sin(angles)
    return (
        jnp.concatenate([cosine, cosine], axis=1),
        jnp.concatenate([-sine_part, sine_part], axis=1),
    )


def turn(head, cosine, sine_part):
    return head * cosine + pltpu.roll(head, HD // 2, 1) * sine_part


def part_of(weight_ref, where, shape):
    rows, columns = shape
    y, core = where[2], where[3]
    return weight_ref[
        pl.ds(pl.multiple_of(y * rows, rows), rows),
        pl.ds(pl.multiple_of(core * columns, columns), columns),
    ]


def cut_weight_kernel(where, weight_ref, *refs):
    refs[-1][...] = part_of(weight_ref, where, refs[-1].shape)


def cut_weight(where, weight, *after):
    part = (weight.shape[0] // 2, weight.shape[1] // 2)
    return pl.pallas_call(
        cut_weight_kernel,
        out_shape=jax.ShapeDtypeStruct(part, jnp.bfloat16),
        in_specs=[SMEM, VMEM] + [ANY] * len(after),
        out_specs=VMEM,
        compiler_params=params(4 * weight.size),
        cost_estimate=cost(0, 3 * weight.size),
    )(where, weight, *after)


def cut_tokens_kernel(n_line, where, x_ref, *refs):
    out_refs = refs[-4:]
    z, x, y = where[0], where[1], where[2]
    width = out_refs[0].shape[2]
    for i in (1, 2, 3, 0):
        for j in range(n_line):
            shard = lax.rem(z - j + n_line, n_line) * 2 + (1 - x if i & 1 else x)
            half = 1 - y if i & 2 else y
            start = pl.multiple_of((shard * 2 + half) * width, width)
            out_refs[i][j] = x_ref[:, pl.ds(start, width)]


def cut_tokens(where, tokens, n_line, *after):
    rows, columns = tokens.shape
    shape = (n_line, rows, columns // (4 * n_line))
    return pl.pallas_call(
        functools.partial(cut_tokens_kernel, n_line),
        out_shape=(jax.ShapeDtypeStruct(shape, jnp.bfloat16),) * 4,
        in_specs=[SMEM, VMEM] + [ANY] * len(after),
        out_specs=(VMEM,) * 4,
        compiler_params=params(4 * tokens.size),
        cost_estimate=cost(0, 4 * tokens.size),
    )(where, tokens, *after)


def project_kernel(n_sets, lines, with_start, n_after, where, *refs):
    n_parts = len(lines)
    refs = list(refs)
    x_refs, refs = refs[: 2 * n_sets], refs[2 * n_sets :]
    w_refs, refs = refs[:n_parts], refs[n_parts:]
    start_refs, refs = (refs[:n_sets], refs[n_sets:]) if with_start else (None, refs)
    outs = refs[n_after:]
    core = where[3]
    tokens = x_refs[0].shape[1]
    for s in range(n_sets):
        for side in range(2):
            x_ref = x_refs[2 * s + side]
            place = pl.ds(pl.multiple_of((1 - core if side else core) * tokens, tokens), tokens)
            total = start_refs[s][place, :] if with_start else None
            for j, w_ref in zip(lines, w_refs):
                term = jnp.dot(x_ref[j], w_ref[...], preferred_element_type=jnp.float32)
                total = term if total is None else total + term
            for out in outs[s::n_sets]:
                out[place, :] = total.astype(out.dtype)


def project(where, sets, lines, pieces, starts, out_types, *after):
    n_line, tokens, rows = sets[0][0].shape
    columns = pieces[0].shape[1]
    n_parts, n_sets = len(lines), len(sets)
    pieces = [pieces[j] for j in lines]
    x_args = [array for pair in sets for array in pair]
    starts = list(starts or [])
    shapes = tuple(
        jax.ShapeDtypeStruct((2 * tokens, columns), t) for t in out_types for _ in sets
    )
    held = n_sets * 4 * tokens * (n_line * rows + 4 * columns) + 2 * n_parts * rows * columns
    return pl.pallas_call(
        functools.partial(project_kernel, n_sets, lines, bool(starts), len(after)),
        out_shape=shapes,
        in_specs=[SMEM]
        + [VMEM] * len(x_args)
        + [VMEM] * (n_parts + len(starts))
        + [ANY] * len(after),
        out_specs=(VMEM,) * len(shapes),
        compiler_params=params(held),
        cost_estimate=cost(4 * n_sets * tokens * n_parts * rows * columns, held),
    )(where, *x_args, *pieces, *starts, *after)


def add_up(refs, span=slice(None)):
    total = refs[0][:, span].astype(jnp.float32)
    for ref in refs[1:]:
        total = total + ref[:, span].astype(jnp.float32)
    return total


def finish_keys_kernel(own_ref, x_ref, y_ref, xy_ref, cosine_ref, sine_ref, out_ref):
    for h in range(out_ref.shape[1] // HD):
        span = slice(h * HD, (h + 1) * HD)
        key = add_up((own_ref, x_ref, y_ref, xy_ref), span)
        out_ref[:, span] = turn(key, cosine_ref[...], sine_ref[...]).astype(jnp.bfloat16)


def finish_values_kernel(own_ref, x_ref, y_ref, xy_ref, out_ref):
    out_ref[...] = add_up((own_ref, x_ref, y_ref, xy_ref)).astype(jnp.bfloat16)


def turn_queries_kernel(q_ref, cosine_ref, sine_ref, after_ref, out_ref):
    for h in range(out_ref.shape[0]):
        query = q_ref[:, h * HD : (h + 1) * HD].astype(jnp.float32)
        out_ref[h] = turn(query, cosine_ref[...], sine_ref[...]).astype(jnp.bfloat16)


def mask_kernel(chip_rows, n_chips, where, lists_ref, out_ref):
    span_rows, tokens = out_ref.shape
    chip, core = where[4], where[3]
    for j in range(n_chips):
        first_key = lax.rem(chip - j + n_chips, n_chips) * chip_rows
        shape = (chip_rows, tokens)
        key = first_key + lax.broadcasted_iota(jnp.int32, shape, 0)
        column = lax.broadcasted_iota(jnp.int32, shape, 1)
        query = chip * chip_rows + core * tokens + column
        key_block, query_row = key // BLOCK, column // BLOCK
        listed = key < 0
        for row in range(lists_ref.shape[0]):
            for entry in range(lists_ref.shape[1]):
                listed = listed | ((key_block == lists_ref[row, entry]) & (query_row == row))
        out_ref[j * chip_rows : (j + 1) * chip_rows, :] = jnp.where(
            listed & (key <= query), 0.0, neg_large
        ).astype(jnp.bfloat16)


def weigh_kernel(n_chips, group, where, q_ref, bias_ref, *refs):
    key_refs, (weight_ref, total_ref, scores) = refs[: 2 * n_chips], refs[2 * n_chips :]
    core = where[3]
    heads_here = key_refs[0].shape[1] // HD
    tokens = q_ref.shape[1]
    span_rows, lanes = scores.shape
    together = lanes // tokens
    scale = HD ** (-0.5) * LOG2E
    square = (tokens, tokens)
    row, column = (lax.broadcasted_iota(jnp.int32, square, axis) for axis in range(2))
    pick = (row == column).astype(jnp.float32).astype(jnp.bfloat16)
    for side in range(2):
        first_head = (1 - core if side else core) * heads_here
        for i in range(heads_here):
            span = slice(i * HD, (i + 1) * HD)
            keys = jnp.concatenate(
                [ref[:, span] for ref in key_refs[side * n_chips : (side + 1) * n_chips]], axis=0
            )
            keys = jnp.concatenate([keys, bias_ref[...]], axis=1)
            pair = side * heads_here + i
            for g in range(0, group, together):
                query = jnp.concatenate(
                    [
                        jnp.concatenate([q_ref[(first_head + i) * group + g + t], pick], axis=1)
                        for t in range(together)
                    ],
                    axis=0,
                )
                scores[...] = lax.dot_general(
                    keys, query, (((1,), (1,)), ((), ())), preferred_element_type=jnp.float32
                )
                top = scores[:8]
                for r in range(8, span_rows, 8):
                    top = jnp.maximum(top, scores[r : r + 8])
                top = jnp.max(top, axis=0, keepdims=True)
                total = jnp.zeros((16, lanes), jnp.float32)
                columns = slice(g * tokens, g * tokens + lanes)
                for r in range(0, span_rows, 16):
                    probabilities = jnp.exp2((scores[r : r + 16] - top) * scale)
                    total = total + probabilities
                    weight_ref[pair, r : r + 16, columns] = probabilities.astype(jnp.bfloat16)
                total_ref[pair, :, columns] = jnp.sum(total, axis=0, keepdims=True)


def mix_kernel(n_chips, group, where, weight_ref, total_ref, *refs):
    value_refs, out_ref, buf, sems = refs[: 2 * n_chips], refs[-3], refs[-2], refs[-1]
    core = where[3]
    heads_here = value_refs[0].shape[1] // HD
    tokens = out_ref.shape[0]
    width = group * HD
    copies = []
    for side in range(2):
        first_head = (1 - core if side else core) * heads_here
        for i in range(heads_here):
            span = slice(i * HD, (i + 1) * HD)
            values = jnp.concatenate(
                [ref[:, span] for ref in value_refs[side * n_chips : (side + 1) * n_chips]],
                axis=0,
            )
            pair = side * heads_here + i
            mixed = jnp.dot(
                values.T, weight_ref[pair], preferred_element_type=jnp.float32
            ) * (1.0 / total_ref[pair])
            for g in range(group):
                buf[pair, :, g * HD : (g + 1) * HD] = mixed[
                    :, g * tokens : (g + 1) * tokens
                ].T.astype(jnp.bfloat16)
            start = pl.multiple_of((first_head + i) * width, width)
            copies.append(
                pltpu.make_async_copy(
                    buf.at[pair], out_ref.at[:, pl.ds(start, width)], sems.at[pair]
                )
            )
            copies[-1].start()
    for copy in copies:
        copy.wait()


def on_device(n_ctx, n_dp, x_tokens, queries, key_weight, value_weight, positions, block_lists):
    n_line, n_chips = n_dp // 2, n_ctx // 2
    tokens_local, query_local = x_tokens[0], queries[0]
    tok_rows, query_width = query_local.shape
    shard_rows, key_width = key_weight.shape
    half_rows, half_columns = shard_rows // 2, key_width // 2
    group = query_width // key_width
    ctx, dp = lax.axis_index("ctx"), lax.axis_index("dp")
    chip, core = ctx // 2, ctx % 2
    y = chip % 2
    where = jnp.stack([dp // 2, dp % 2, y, core, chip]).astype(jnp.int32)

    def over_core(array):
        return lax.ppermute(array, "ctx", [(i, i ^ 1) for i in range(n_ctx)])

    def over_y(array):
        return lax.ppermute(array, "ctx", [(i, i ^ 2) for i in range(n_ctx)])

    def over_x(array):
        return lax.ppermute(array, "dp", [(i, i ^ 1) for i in range(n_dp)])

    def over_z(array, step):
        return lax.ppermute(array, "dp", [(i, (i + 2 * step) % n_dp) for i in range(n_dp)])

    def over_xy(array):
        pairs = [
            (i * n_dp + d, (i ^ 2) * n_dp + (d ^ 1)) for i in range(n_ctx) for d in range(n_dp)
        ]
        return lax.ppermute(array, ("ctx", "dp"), pairs)

    def from_chip(array, step):
        return lax.ppermute(array, "ctx", [(i, (i + 2 * step) % n_ctx) for i in range(n_ctx)])

    up = n_line // 2

    def gather_pieces(own, late, after):
        came = [None] * n_line
        came[0] = own
        for j in range(1, up + 1):
            k = n_line - j
            if k > up:
                came[k] = over_z(came[(k + 1) % n_line], -1)
            before = came[j - 1]
            if j == up and (late or after):
                before = lax.optimization_barrier(
                    (before, *([came[up + 1]] if late else []), *after)
                )[0]
            came[j] = over_z(before, 1)
        return came

    cuts = cut_tokens(where, tokens_local, n_line)
    key_own = cut_weight(where, key_weight, cuts[0])
    token_pos = positions[0]
    pos_pair = jnp.stack([token_pos, over_core(positions)[0]])
    pos_chip = jnp.where(core == 0, pos_pair, pos_pair[::-1]).reshape(-1)
    cosine, sine_part = rope_tables(pos_chip)
    own_rows = core * tok_rows
    query_cosine = lax.dynamic_slice_in_dim(cosine, own_rows, tok_rows, 0)
    query_sine = lax.dynamic_slice_in_dim(sine_part, own_rows, tok_rows, 0)
    n_heads = query_width // HD
    query_rot = pl.pallas_call(
        turn_queries_kernel,
        out_shape=jax.ShapeDtypeStruct((n_heads, tok_rows, HD), jnp.bfloat16),
        in_specs=[VMEM] * 3 + [ANY],
        out_specs=VMEM,
        compiler_params=params(4 * query_local.size),
        cost_estimate=cost(3 * query_local.size, 4 * query_local.size),
    )(query_local, query_cosine, query_sine, key_own)

    chip_rows = 2 * tok_rows
    bias = pl.pallas_call(
        functools.partial(mask_kernel, chip_rows, n_chips),
        out_shape=jax.ShapeDtypeStruct((n_chips * chip_rows, tok_rows), jnp.bfloat16),
        in_specs=[SMEM, SMEM],
        out_specs=VMEM,
        compiler_params=params(16 * chip_rows * tok_rows),
        cost_estimate=cost(20 * n_chips * chip_rows * tok_rows, 0),
    )(where, block_lists[0])

    key_pieces = gather_pieces(key_own, True, [bias, cosine, sine_part])
    held = [cuts[0], over_x(cuts[1]), over_y(cuts[2]), over_xy(cuts[3])]
    value_own = cut_weight(where, value_weight, cuts[0])
    value_pieces = gather_pieces(value_own, False, [])

    held[1:] = lax.optimization_barrier(
        (*held[1:], key_pieces[up], value_pieces[1], query_rot)
    )[:3]
    sets = [(array, over_core(array)) for array in held]

    f32, bf16 = jnp.float32, jnp.bfloat16
    every = list(range(n_line))
    key_parts = project(
        where, sets, every, key_pieces, None, (f32,), key_own
    )
    key_here = pl.pallas_call(
        finish_keys_kernel,
        out_shape=jax.ShapeDtypeStruct(key_parts[0].shape, bf16),
        in_specs=[VMEM] * 6,
        out_specs=VMEM,
        compiler_params=params(26 * key_parts[0].size),
        cost_estimate=cost(6 * key_parts[0].size, 26 * key_parts[0].size),
    )(
        key_parts[0], over_x(key_parts[1]), over_y(key_parts[2]), over_xy(key_parts[3]),
        cosine, sine_part,
    )
    keys = [key_here] + [from_chip(key_here, j) for j in range(1, n_chips)]
    keys += [over_core(array) for array in keys]

    early = [j for j in every if j != up]
    early_values = project(where, sets, early, value_pieces, None, (f32,), key_parts[0])
    value_parts = project(where, sets, [up], value_pieces, early_values, (bf16,))
    value_here = pl.pallas_call(
        finish_values_kernel,
        out_shape=jax.ShapeDtypeStruct(value_parts[0].shape, bf16),
        in_specs=[VMEM] * 4,
        out_specs=VMEM,
        compiler_params=params(10 * value_parts[0].size),
        cost_estimate=cost(3 * value_parts[0].size, 10 * value_parts[0].size),
    )(value_parts[0], over_x(value_parts[1]), over_y(value_parts[2]), over_xy(value_parts[3]))
    values = [value_here] + [from_chip(value_here, j) for j in range(1, n_chips)]
    values += [over_core(array) for array in values]

    span_rows = n_chips * chip_rows
    pairs, lanes = 2 * (keys[0].shape[1] // HD), group * tok_rows
    held = 2 * tok_rows * (query_width + n_heads * span_rows)
    weights, totals = pl.pallas_call(
        functools.partial(weigh_kernel, n_chips, group),
        out_shape=(
            jax.ShapeDtypeStruct((pairs, span_rows, lanes), bf16),
            jax.ShapeDtypeStruct((pairs, 1, lanes), f32),
        ),
        in_specs=[SMEM] + [VMEM] * (2 + len(keys)),
        out_specs=(VMEM, VMEM),
        scratch_shapes=[pltpu.VMEM((span_rows, 2 * tok_rows), f32)],
        compiler_params=params(held + 10 * bias.size + 4 * span_rows * key_width),
        cost_estimate=cost(
            2 * tok_rows * query_width * span_rows, held, tok_rows * n_heads * span_rows
        ),
    )(where, query_rot, bias, *keys)
    mixed = pl.pallas_call(
        functools.partial(mix_kernel, n_chips, group),
        out_shape=jax.ShapeDtypeStruct((tok_rows, query_width), bf16),
        in_specs=[SMEM] + [VMEM] * (2 + len(values)),
        out_specs=ANY,
        scratch_shapes=[
            pltpu.VMEM((pairs, tok_rows, group * HD), bf16),
            pltpu.SemaphoreType.DMA((pairs,)),
        ],
        compiler_params=params(held + 4 * span_rows * key_width),
        cost_estimate=cost(2 * tok_rows * query_width * span_rows, held),
    )(where, weights, totals, *values)
    return mixed[None]


def solution(mesh):
    return jax.shard_map(
        functools.partial(on_device, mesh.shape["ctx"], mesh.shape["dp"]),
        mesh=mesh,
        in_specs=(
            P("dp", "ctx", None),
            P("dp", "ctx", None),
            P("dp", None),
            P("dp", None),
            P("dp", "ctx"),
            P("dp", "ctx", None),
        ),
        out_specs=P("dp", "ctx", None),
        check_vma=False,
    )
```

```python
import functools
import math

import jax
import jax.numpy as jnp
from jax import lax
from jax.experimental import pallas as pl
from jax.experimental.pallas import tpu as pltpu
from jax.sharding import PartitionSpec as P

HD = 128
BLOCK = 64
LOG2E = 1.4426950408889634

neg_large = -1e30
HEADROOM = 2 * 1024 * 1024
ANY = pl.BlockSpec(memory_space=pl.ANY)
VMEM = pl.BlockSpec(memory_space=pltpu.VMEM)
SMEM = pl.BlockSpec(memory_space=pltpu.SMEM)


def params(held):
    return pltpu.CompilerParams(vmem_limit_bytes=held + HEADROOM)


def cost(flops, bytes_accessed, transcendentals=0):
    return pl.CostEstimate(
        flops=flops, bytes_accessed=bytes_accessed, transcendentals=transcendentals
    )


def rope_periods(half_width):
    return jnp.array(
        [
            int(2.0 * math.pi * 500000.0 ** (column / half_width) + 0.5)
            for column in range(half_width)
        ],
        jnp.int32,
    )


def rope_tables(token_pos):
    half_width = HD // 2
    periods = rope_periods(half_width)
    turn_counts = jnp.remainder(token_pos[:, None], periods[None, :])
    angles = 2.0 * math.pi * turn_counts.astype(jnp.float32) / periods.astype(jnp.float32)
    cosine = jnp.cos(angles)
    sine_part = jnp.sin(angles)
    return (
        jnp.concatenate([cosine, cosine], axis=1),
        jnp.concatenate([-sine_part, sine_part], axis=1),
    )


def turn(head, cosine, sine_part):
    return head * cosine + pltpu.roll(head, HD // 2, 1) * sine_part


def part_of(weight_ref, where, shape):
    rows, columns = shape
    y, core = where[2], where[3]
    return weight_ref[
        pl.ds(pl.multiple_of(y * rows, rows), rows),
        pl.ds(pl.multiple_of(core * columns, columns), columns),
    ]


def cut_weight_kernel(where, weight_ref, *refs):
    refs[-1][...] = part_of(weight_ref, where, refs[-1].shape)


def cut_weight(where, weight, *after):
    part = (weight.shape[0] // 2, weight.shape[1] // 2)
    return pl.pallas_call(
        cut_weight_kernel,
        out_shape=jax.ShapeDtypeStruct(part, jnp.bfloat16),
        in_specs=[SMEM, VMEM] + [ANY] * len(after),
        out_specs=VMEM,
        compiler_params=params(4 * weight.size),
        cost_estimate=cost(0, 3 * weight.size),
    )(where, weight, *after)


def cut_tokens_kernel(n_line, where, x_ref, *refs):
    out_refs = refs[-4:]
    z, x, y = where[0], where[1], where[2]
    width = out_refs[0].shape[2]
    for i in (1, 2, 3, 0):
        for j in range(n_line):
            shard = lax.rem(z - j + n_line, n_line) * 2 + (1 - x if i & 1 else x)
            half = 1 - y if i & 2 else y
            start = pl.multiple_of((shard * 2 + half) * width, width)
            out_refs[i][j] = x_ref[:, pl.ds(start, width)]


def cut_tokens(where, tokens, n_line, *after):
    rows, columns = tokens.shape
    shape = (n_line, rows, columns // (4 * n_line))
    return pl.pallas_call(
        functools.partial(cut_tokens_kernel, n_line),
        out_shape=(jax.ShapeDtypeStruct(shape, jnp.bfloat16),) * 4,
        in_specs=[SMEM, VMEM] + [ANY] * len(after),
        out_specs=(VMEM,) * 4,
        compiler_params=params(4 * tokens.size),
        cost_estimate=cost(0, 4 * tokens.size),
    )(where, tokens, *after)


def project_kernel(n_sets, lines, with_start, n_after, where, *refs):
    n_parts = len(lines)
    refs = list(refs)
    x_refs, refs = refs[: 2 * n_sets], refs[2 * n_sets :]
    w_refs, refs = refs[:n_parts], refs[n_parts:]
    start_refs, refs = (refs[:n_sets], refs[n_sets:]) if with_start else (None, refs)
    outs = refs[n_after:]
    core = where[3]
    tokens = x_refs[0].shape[1]
    for s in range(n_sets):
        for side in range(2):
            x_ref = x_refs[2 * s + side]
            place = pl.ds(pl.multiple_of((1 - core if side else core) * tokens, tokens), tokens)
            total = start_refs[s][place, :] if with_start else None
            for j, w_ref in zip(lines, w_refs):
                term = jnp.dot(x_ref[j], w_ref[...], preferred_element_type=jnp.float32)
                total = term if total is None else total + term
            for out in outs[s::n_sets]:
                out[place, :] = total.astype(out.dtype)


def project(where, sets, lines, pieces, starts, out_types, *after):
    n_line, tokens, rows = sets[0][0].shape
    columns = pieces[0].shape[1]
    n_parts, n_sets = len(lines), len(sets)
    pieces = [pieces[j] for j in lines]
    x_args = [array for pair in sets for array in pair]
    starts = list(starts or [])
    shapes = tuple(
        jax.ShapeDtypeStruct((2 * tokens, columns), t) for t in out_types for _ in sets
    )
    held = n_sets * 4 * tokens * (n_line * rows + 4 * columns) + 2 * n_parts * rows * columns
    return pl.pallas_call(
        functools.partial(project_kernel, n_sets, lines, bool(starts), len(after)),
        out_shape=shapes,
        in_specs=[SMEM]
        + [VMEM] * len(x_args)
        + [VMEM] * (n_parts + len(starts))
        + [ANY] * len(after),
        out_specs=(VMEM,) * len(shapes),
        compiler_params=params(held),
        cost_estimate=cost(4 * n_sets * tokens * n_parts * rows * columns, held),
    )(where, *x_args, *pieces, *starts, *after)


def add_up(refs, span=slice(None)):
    total = refs[0][:, span].astype(jnp.float32)
    for ref in refs[1:]:
        total = total + ref[:, span].astype(jnp.float32)
    return total


def finish_keys_kernel(own_ref, x_ref, y_ref, xy_ref, cosine_ref, sine_ref, out_ref):
    for h in range(out_ref.shape[1] // HD):
        span = slice(h * HD, (h + 1) * HD)
        key = add_up((own_ref, x_ref, y_ref, xy_ref), span)
        out_ref[:, span] = turn(key, cosine_ref[...], sine_ref[...]).astype(jnp.bfloat16)


def finish_values_kernel(own_ref, x_ref, y_ref, xy_ref, out_ref):
    out_ref[...] = add_up((own_ref, x_ref, y_ref, xy_ref)).astype(jnp.bfloat16)


def turn_queries_kernel(where, q_ref, cosine_ref, sine_ref, after_ref, out_ref):
    half = out_ref.shape[0] // 2
    core = where[3]
    for h in range(2 * half):
        side = 1 - core if h // half else core
        start = pl.multiple_of((side * half + h % half) * HD, HD)
        query = q_ref[:, pl.ds(start, HD)].astype(jnp.float32)
        out_ref[h] = turn(query, cosine_ref[...], sine_ref[...]).astype(jnp.bfloat16)


def mask_kernel(chip_rows, n_chips, where, lists_ref, *refs):
    out_ref = refs[-1]
    tokens = out_ref.shape[1]
    chip, core = where[4], where[3]
    shape = (BLOCK, tokens)
    row, column = (lax.broadcasted_iota(jnp.int32, shape, axis) for axis in range(2))
    ahead = row - column
    first_query = chip * chip_rows + core * tokens
    for j in range(n_chips):
        for b in range(chip_rows // BLOCK):
            first_key = lax.rem(chip - j + n_chips, n_chips) * chip_rows + b * BLOCK
            listed = ahead > tokens + BLOCK
            for q in range(lists_ref.shape[0]):
                found = lists_ref[q, 0] == first_key // BLOCK
                for entry in range(1, lists_ref.shape[1]):
                    found = found | (lists_ref[q, entry] == first_key // BLOCK)
                limit = jnp.where(found, first_query - first_key, -tokens - BLOCK)
                listed = listed | ((column // BLOCK == q) & (ahead <= limit))
            rows = slice(j * chip_rows + b * BLOCK, j * chip_rows + (b + 1) * BLOCK)
            out_ref[rows, :] = jnp.where(listed, 0.0, neg_large).astype(jnp.bfloat16)


def weigh_kernel(first, group, q_ref, bias_ref, *refs):
    key_refs, (weight_ref, total_ref, scores) = refs[:-3], refs[-3:]
    tokens = q_ref.shape[1]
    span_rows, lanes = scores.shape
    together = lanes // tokens
    scale = HD ** (-0.5) * LOG2E
    square = (tokens, tokens)
    row, column = (lax.broadcasted_iota(jnp.int32, square, axis) for axis in range(2))
    pick = (row == column).astype(jnp.float32).astype(jnp.bfloat16)
    for pair in range(weight_ref.shape[0]):
        span = slice(pair * HD, (pair + 1) * HD)
        keys = jnp.concatenate([ref[:, span] for ref in key_refs], axis=0)
        keys = jnp.concatenate([keys, bias_ref[...]], axis=1)
        for g in range(0, group, together):
            head = first + pair * group + g
            query = jnp.concatenate(
                [jnp.concatenate([q_ref[head + t], pick], axis=1) for t in range(together)],
                axis=0,
            )
            scores[...] = lax.dot_general(
                keys, query, (((1,), (1,)), ((), ())), preferred_element_type=jnp.float32
            )
            top = scores[:8]
            for r in range(8, span_rows, 8):
                top = jnp.maximum(top, scores[r : r + 8])
            top = jnp.max(top, axis=0, keepdims=True)
            total = jnp.zeros((16, lanes), jnp.float32)
            columns = slice(g * tokens, g * tokens + lanes)
            for r in range(0, span_rows, 16):
                probabilities = jnp.exp2((scores[r : r + 16] - top) * scale)
                total = total + probabilities
                weight_ref[pair, r : r + 16, columns] = probabilities.astype(jnp.bfloat16)
            total_ref[pair, :, columns] = jnp.sum(total, axis=0, keepdims=True)


def weigh(query_rot, bias, keys, first, group):
    _, tokens, _ = query_rot.shape
    span_rows = bias.shape[0]
    pairs, lanes = keys[0].shape[1] // HD, group * tokens
    held = 2 * query_rot.size + 10 * bias.size + 2 * pairs * span_rows * lanes
    return pl.pallas_call(
        functools.partial(weigh_kernel, first, group),
        out_shape=(
            jax.ShapeDtypeStruct((pairs, span_rows, lanes), jnp.bfloat16),
            jax.ShapeDtypeStruct((pairs, 1, lanes), jnp.float32),
        ),
        in_specs=[VMEM] * (2 + len(keys)),
        out_specs=(VMEM, VMEM),
        scratch_shapes=[pltpu.VMEM((span_rows, 2 * tokens), jnp.float32)],
        compiler_params=params(held + 4 * len(keys) * keys[0].size),
        cost_estimate=cost(
            2 * pairs * span_rows * lanes * HD, held, pairs * span_rows * lanes
        ),
    )(query_rot, bias, *keys)


def mix_kernel(n_chips, group, where, *refs):
    weight_refs, total_refs, refs = refs[:2], refs[2:4], refs[4:]
    value_refs, out_ref, buf, sems = refs[: 2 * n_chips], refs[-3], refs[-2], refs[-1]
    core = where[3]
    heads_here = value_refs[0].shape[1] // HD
    tokens = out_ref.shape[0]
    width = group * HD
    copies = []
    for side in range(2):
        first_head = (1 - core if side else core) * heads_here
        for i in range(heads_here):
            span = slice(i * HD, (i + 1) * HD)
            values = jnp.concatenate(
                [ref[:, span] for ref in value_refs[side * n_chips : (side + 1) * n_chips]],
                axis=0,
            )
            pair = side * heads_here + i
            mixed = jnp.dot(
                values.T, weight_refs[side][i], preferred_element_type=jnp.float32
            ) * (1.0 / total_refs[side][i])
            for g in range(group):
                buf[pair, :, g * HD : (g + 1) * HD] = mixed[
                    :, g * tokens : (g + 1) * tokens
                ].T.astype(jnp.bfloat16)
            start = pl.multiple_of((first_head + i) * width, width)
            copies.append(
                pltpu.make_async_copy(
                    buf.at[pair], out_ref.at[:, pl.ds(start, width)], sems.at[pair]
                )
            )
            copies[-1].start()
    for copy in copies:
        copy.wait()


def on_device(n_ctx, n_dp, x_tokens, queries, key_weight, value_weight, positions, block_lists):
    n_line, n_chips = n_dp // 2, n_ctx // 2
    tokens_local, query_local = x_tokens[0], queries[0]
    tok_rows, query_width = query_local.shape
    shard_rows, key_width = key_weight.shape
    half_rows, half_columns = shard_rows // 2, key_width // 2
    group = query_width // key_width
    ctx, dp = lax.axis_index("ctx"), lax.axis_index("dp")
    chip, core = ctx // 2, ctx % 2
    y = chip % 2
    where = jnp.stack([dp // 2, dp % 2, y, core, chip]).astype(jnp.int32)

    def over_core(array):
        return lax.ppermute(array, "ctx", [(i, i ^ 1) for i in range(n_ctx)])

    def over_y(array):
        return lax.ppermute(array, "ctx", [(i, i ^ 2) for i in range(n_ctx)])

    def over_x(array):
        return lax.ppermute(array, "dp", [(i, i ^ 1) for i in range(n_dp)])

    def over_z(array, step):
        return lax.ppermute(array, "dp", [(i, (i + 2 * step) % n_dp) for i in range(n_dp)])

    def over_xy(array):
        pairs = [
            (i * n_dp + d, (i ^ 2) * n_dp + (d ^ 1)) for i in range(n_ctx) for d in range(n_dp)
        ]
        return lax.ppermute(array, ("ctx", "dp"), pairs)

    def from_chip(array, step):
        return lax.ppermute(array, "ctx", [(i, (i + 2 * step) % n_ctx) for i in range(n_ctx)])

    up = n_line // 2

    def gather_pieces(own, late, after):
        came = [None] * n_line
        came[0] = own
        for j in range(1, up + 1):
            k = n_line - j
            if k > up:
                came[k] = over_z(came[(k + 1) % n_line], -1)
            before = came[j - 1]
            if j == up and (late or after):
                before = lax.optimization_barrier(
                    (before, *([came[up + 1]] if late else []), *after)
                )[0]
            came[j] = over_z(before, 1)
        return came

    key_own = cut_weight(where, key_weight)
    cuts = cut_tokens(where, tokens_local, n_line, key_own)
    key_pieces = gather_pieces(key_own, True, [])
    held = [cuts[0], over_x(cuts[1]), over_y(cuts[2]), over_xy(cuts[3])]
    value_own = cut_weight(where, value_weight, cuts[0])
    value_pieces = gather_pieces(value_own, False, [])

    positions = lax.optimization_barrier((positions, key_pieces[1]))[0]
    token_pos = positions[0]
    pos_pair = jnp.stack([token_pos, over_core(positions)[0]])
    pos_chip = jnp.where(core == 0, pos_pair, pos_pair[::-1]).reshape(-1)
    cosine, sine_part = rope_tables(pos_chip)
    own_rows = core * tok_rows
    query_cosine = lax.dynamic_slice_in_dim(cosine, own_rows, tok_rows, 0)
    query_sine = lax.dynamic_slice_in_dim(sine_part, own_rows, tok_rows, 0)
    n_heads = query_width // HD
    query_rot = pl.pallas_call(
        turn_queries_kernel,
        out_shape=jax.ShapeDtypeStruct((n_heads, tok_rows, HD), jnp.bfloat16),
        in_specs=[SMEM] + [VMEM] * 3 + [ANY],
        out_specs=VMEM,
        compiler_params=params(4 * query_local.size),
        cost_estimate=cost(3 * query_local.size, 4 * query_local.size),
    )(where, query_local, query_cosine, query_sine, key_pieces[1])

    chip_rows = 2 * tok_rows
    bias = pl.pallas_call(
        functools.partial(mask_kernel, chip_rows, n_chips),
        out_shape=jax.ShapeDtypeStruct((n_chips * chip_rows, tok_rows), jnp.bfloat16),
        in_specs=[SMEM, SMEM, ANY],
        out_specs=VMEM,
        compiler_params=params(16 * chip_rows * tok_rows),
        cost_estimate=cost(20 * n_chips * chip_rows * tok_rows, 0),
    )(where, block_lists[0], key_pieces[up])

    held[1:3] = lax.optimization_barrier((*held[1:3], key_pieces[up], value_pieces[1], query_rot, bias, cosine, sine_part))[:2]
    f32, bf16 = jnp.float32, jnp.bfloat16
    every = list(range(n_line))
    sets = [(array, over_core(array)) for array in held[:3]]
    key_x, key_y = project(where, sets[1:], every, key_pieces, None, (f32,), bias, cosine, sine_part)
    *held[3:], _ = lax.optimization_barrier((held[3], held[1], value_pieces[-1]))
    sets.append((held[3], over_core(held[3])))
    key_own_part, key_xy = project(
        where, [sets[0], sets[3]], every, key_pieces, None, (f32,), key_x
    )
    key_parts = (key_own_part, key_x, key_y, key_xy)
    key_here = pl.pallas_call(
        finish_keys_kernel,
        out_shape=jax.ShapeDtypeStruct(key_parts[0].shape, bf16),
        in_specs=[VMEM] * 6,
        out_specs=VMEM,
        compiler_params=params(26 * key_parts[0].size),
        cost_estimate=cost(6 * key_parts[0].size, 26 * key_parts[0].size),
    )(
        key_parts[0], over_x(key_parts[1]), over_y(key_parts[2]), over_xy(key_parts[3]),
        cosine, sine_part,
    )
    keys = [key_here] + [from_chip(key_here, j) for j in range(1, n_chips)]
    keys_other = [over_core(array) for array in keys]

    early = [j for j in every if j != up]
    early_values = project(where, sets, early, value_pieces, None, (f32,), key_parts[0])
    value_parts = project(where, sets, [up], value_pieces, early_values, (bf16,))
    value_here = pl.pallas_call(
        finish_values_kernel,
        out_shape=jax.ShapeDtypeStruct(value_parts[0].shape, bf16),
        in_specs=[VMEM] * 4,
        out_specs=VMEM,
        compiler_params=params(10 * value_parts[0].size),
        cost_estimate=cost(3 * value_parts[0].size, 10 * value_parts[0].size),
    )(value_parts[0], over_x(value_parts[1]), over_y(value_parts[2]), over_xy(value_parts[3]))
    weights, totals = weigh(query_rot, bias, keys, 0, group)
    values = [value_here] + [from_chip(value_here, j) for j in range(1, n_chips)]
    *values, weights = lax.optimization_barrier((*values, weights))
    values += [over_core(array) for array in values]
    weights_other, totals_other = weigh(query_rot, bias, keys_other, n_heads // 2, group)

    span_rows = n_chips * chip_rows
    pairs = n_heads // group
    held = 2 * tok_rows * (query_width + n_heads * span_rows)
    mixed = pl.pallas_call(
        functools.partial(mix_kernel, n_chips, group),
        out_shape=jax.ShapeDtypeStruct((tok_rows, query_width), bf16),
        in_specs=[SMEM] + [VMEM] * (4 + len(values)),
        out_specs=ANY,
        scratch_shapes=[
            pltpu.VMEM((pairs, tok_rows, group * HD), bf16),
            pltpu.SemaphoreType.DMA((pairs,)),
        ],
        compiler_params=params(held + 4 * span_rows * key_width),
        cost_estimate=cost(2 * tok_rows * query_width * span_rows, held),
    )(where, weights, weights_other, totals, totals_other, *values)
    return mixed[None]


def solution(mesh):
    return jax.shard_map(
        functools.partial(on_device, mesh.shape["ctx"], mesh.shape["dp"]),
        mesh=mesh,
        in_specs=(
            P("dp", "ctx", None),
            P("dp", "ctx", None),
            P("dp", None),
            P("dp", None),
            P("dp", "ctx"),
            P("dp", "ctx", None),
        ),
        out_specs=P("dp", "ctx", None),
        check_vma=False,
    )
```

```python
import functools
import math

import jax
import jax.numpy as jnp
from jax import lax
from jax.experimental import pallas as pl
from jax.experimental.pallas import tpu as pltpu
from jax.sharding import PartitionSpec as P

HD = 128
BLOCK = 64
LOG2E = 1.4426950408889634

neg_large = -1e30
HEADROOM = 2 * 1024 * 1024
ANY = pl.BlockSpec(memory_space=pl.ANY)
VMEM = pl.BlockSpec(memory_space=pltpu.VMEM)
SMEM = pl.BlockSpec(memory_space=pltpu.SMEM)


def params(held):
    return pltpu.CompilerParams(vmem_limit_bytes=held + HEADROOM)


def cost(flops, bytes_accessed, transcendentals=0):
    return pl.CostEstimate(
        flops=flops, bytes_accessed=bytes_accessed, transcendentals=transcendentals
    )


def rope_periods(half_width):
    return jnp.array(
        [
            int(2.0 * math.pi * 500000.0 ** (column / half_width) + 0.5)
            for column in range(half_width)
        ],
        jnp.int32,
    )


def rope_tables(token_pos):
    half_width = HD // 2
    periods = rope_periods(half_width)
    turn_counts = jnp.remainder(token_pos[:, None], periods[None, :])
    angles = 2.0 * math.pi * turn_counts.astype(jnp.float32) / periods.astype(jnp.float32)
    cosine = jnp.cos(angles)
    sine_part = jnp.sin(angles)
    return (
        jnp.concatenate([cosine, cosine], axis=1),
        jnp.concatenate([-sine_part, sine_part], axis=1),
    )


def turn(head, cosine, sine_part):
    return head * cosine + pltpu.roll(head, HD // 2, 1) * sine_part


def part_of(weight_ref, where, shape):
    rows, columns = shape
    y, core = where[2], where[3]
    return weight_ref[
        pl.ds(pl.multiple_of(y * rows, rows), rows),
        pl.ds(pl.multiple_of(core * columns, columns), columns),
    ]


def cut_weight_kernel(where, weight_ref, *refs):
    refs[-1][...] = part_of(weight_ref, where, refs[-1].shape)


def cut_weight(where, weight, *after):
    part = (weight.shape[0] // 2, weight.shape[1] // 2)
    return pl.pallas_call(
        cut_weight_kernel,
        out_shape=jax.ShapeDtypeStruct(part, jnp.bfloat16),
        in_specs=[SMEM, VMEM] + [ANY] * len(after),
        out_specs=VMEM,
        compiler_params=params(4 * weight.size),
        cost_estimate=cost(0, 3 * weight.size),
    )(where, weight, *after)


def cut_tokens_kernel(n_line, where, x_ref, *refs):
    out_refs = refs[-4:]
    z, x, y = where[0], where[1], where[2]
    width = out_refs[0].shape[2]
    for i in (1, 2, 3, 0):
        for j in range(n_line):
            shard = lax.rem(z - j + n_line, n_line) * 2 + (1 - x if i & 1 else x)
            half = 1 - y if i & 2 else y
            start = pl.multiple_of((shard * 2 + half) * width, width)
            out_refs[i][j] = x_ref[:, pl.ds(start, width)]


def cut_tokens(where, tokens, n_line, *after):
    rows, columns = tokens.shape
    shape = (n_line, rows, columns // (4 * n_line))
    return pl.pallas_call(
        functools.partial(cut_tokens_kernel, n_line),
        out_shape=(jax.ShapeDtypeStruct(shape, jnp.bfloat16),) * 4,
        in_specs=[SMEM, VMEM] + [ANY] * len(after),
        out_specs=(VMEM,) * 4,
        compiler_params=pltpu.CompilerParams(vmem_limit_bytes=52 * 1024 * 1024),
        cost_estimate=cost(0, 4 * tokens.size),
    )(where, tokens, *after)


def project_kernel(n_sets, lines, with_start, n_after, where, *refs):
    n_parts = len(lines)
    refs = list(refs)
    x_refs, refs = refs[: 2 * n_sets], refs[2 * n_sets :]
    w_refs, refs = refs[:n_parts], refs[n_parts:]
    start_refs, refs = (refs[:n_sets], refs[n_sets:]) if with_start else (None, refs)
    outs = refs[n_after:]
    core = where[3]
    tokens = x_refs[0].shape[1]
    for s in range(n_sets):
        for side in range(2):
            x_ref = x_refs[2 * s + side]
            place = pl.ds(pl.multiple_of((1 - core if side else core) * tokens, tokens), tokens)
            total = start_refs[s][place, :] if with_start else None
            for j, w_ref in zip(lines, w_refs):
                term = jnp.dot(x_ref[j], w_ref[...], preferred_element_type=jnp.float32)
                total = term if total is None else total + term
            for out in outs[s::n_sets]:
                out[place, :] = total.astype(out.dtype)


def project(where, sets, lines, pieces, starts, out_types, *after):
    n_line, tokens, rows = sets[0][0].shape
    columns = pieces[0].shape[1]
    n_parts, n_sets = len(lines), len(sets)
    pieces = [pieces[j] for j in lines]
    x_args = [array for pair in sets for array in pair]
    starts = list(starts or [])
    shapes = tuple(
        jax.ShapeDtypeStruct((2 * tokens, columns), t) for t in out_types for _ in sets
    )
    held = n_sets * 4 * tokens * (n_line * rows + 4 * columns) + 2 * n_parts * rows * columns
    return pl.pallas_call(
        functools.partial(project_kernel, n_sets, lines, bool(starts), len(after)),
        out_shape=shapes,
        in_specs=[SMEM]
        + [VMEM] * len(x_args)
        + [VMEM] * (n_parts + len(starts))
        + [ANY] * len(after),
        out_specs=(VMEM,) * len(shapes),
        compiler_params=params(held),
        cost_estimate=cost(4 * n_sets * tokens * n_parts * rows * columns, held),
    )(where, *x_args, *pieces, *starts, *after)


def add_up(refs, span=slice(None)):
    total = refs[0][:, span].astype(jnp.float32)
    for ref in refs[1:]:
        total = total + ref[:, span].astype(jnp.float32)
    return total


def finish_keys_kernel(own_ref, x_ref, y_ref, xy_ref, cosine_ref, sine_ref, out_ref):
    for h in range(out_ref.shape[1] // HD):
        span = slice(h * HD, (h + 1) * HD)
        key = add_up((own_ref, x_ref, y_ref, xy_ref), span)
        out_ref[:, span] = turn(key, cosine_ref[...], sine_ref[...]).astype(jnp.bfloat16)


def finish_values_kernel(own_ref, x_ref, y_ref, xy_ref, out_ref):
    out_ref[...] = add_up((own_ref, x_ref, y_ref, xy_ref)).astype(jnp.bfloat16)


def turn_queries_kernel(where, q_ref, cosine_ref, sine_ref, after_ref, out_ref):
    half = out_ref.shape[0] // 2
    core = where[3]
    for h in range(2 * half):
        side = 1 - core if h // half else core
        start = pl.multiple_of((side * half + h % half) * HD, HD)
        query = q_ref[:, pl.ds(start, HD)].astype(jnp.float32)
        out_ref[h] = turn(query, cosine_ref[...], sine_ref[...]).astype(jnp.bfloat16)


def mask_kernel(chip_rows, n_chips, where, lists_ref, *refs):
    out_ref = refs[-1]
    tokens = out_ref.shape[1]
    chip, core = where[4], where[3]
    shape = (BLOCK, tokens)
    row, column = (lax.broadcasted_iota(jnp.int32, shape, axis) for axis in range(2))
    ahead = row - column
    first_query = chip * chip_rows + core * tokens
    for j in range(n_chips):
        for b in range(chip_rows // BLOCK):
            first_key = lax.rem(chip - j + n_chips, n_chips) * chip_rows + b * BLOCK
            listed = ahead > tokens + BLOCK
            for q in range(lists_ref.shape[0]):
                found = lists_ref[q, 0] == first_key // BLOCK
                for entry in range(1, lists_ref.shape[1]):
                    found = found | (lists_ref[q, entry] == first_key // BLOCK)
                limit = jnp.where(found, first_query - first_key, -tokens - BLOCK)
                listed = listed | ((column // BLOCK == q) & (ahead <= limit))
            rows = slice(j * chip_rows + b * BLOCK, j * chip_rows + (b + 1) * BLOCK)
            out_ref[rows, :] = jnp.where(listed, 0.0, neg_large).astype(jnp.bfloat16)


def weigh_kernel(first, group, q_ref, bias_ref, *refs):
    key_refs, (weight_ref, total_ref, scores) = refs[:-3], refs[-3:]
    tokens = q_ref.shape[1]
    span_rows, lanes = scores.shape
    together = lanes // tokens
    scale = HD ** (-0.5) * LOG2E
    square = (tokens, tokens)
    row, column = (lax.broadcasted_iota(jnp.int32, square, axis) for axis in range(2))
    pick = (row == column).astype(jnp.float32).astype(jnp.bfloat16)
    for pair in range(weight_ref.shape[0]):
        span = slice(pair * HD, (pair + 1) * HD)
        keys = jnp.concatenate([ref[:, span] for ref in key_refs], axis=0)
        keys = jnp.concatenate([keys, bias_ref[...]], axis=1)
        for g in range(0, group, together):
            head = first + pair * group + g
            query = jnp.concatenate(
                [jnp.concatenate([q_ref[head + t], pick], axis=1) for t in range(together)],
                axis=0,
            )
            scores[...] = lax.dot_general(
                keys, query, (((1,), (1,)), ((), ())), preferred_element_type=jnp.float32
            )
            top = scores[:8]
            for r in range(8, span_rows, 8):
                top = jnp.maximum(top, scores[r : r + 8])
            top = jnp.max(top, axis=0, keepdims=True)
            total = jnp.zeros((16, lanes), jnp.float32)
            columns = slice(g * tokens, g * tokens + lanes)
            for r in range(0, span_rows, 16):
                probabilities = jnp.exp2((scores[r : r + 16] - top) * scale)
                total = total + probabilities
                weight_ref[pair, r : r + 16, columns] = probabilities.astype(jnp.bfloat16)
            total_ref[pair, :, columns] = jnp.sum(total, axis=0, keepdims=True)


def weigh(query_rot, bias, keys, first, group):
    _, tokens, _ = query_rot.shape
    span_rows = bias.shape[0]
    pairs, lanes = keys[0].shape[1] // HD, group * tokens
    held = 2 * query_rot.size + 10 * bias.size + 2 * pairs * span_rows * lanes
    return pl.pallas_call(
        functools.partial(weigh_kernel, first, group),
        out_shape=(
            jax.ShapeDtypeStruct((pairs, span_rows, lanes), jnp.bfloat16),
            jax.ShapeDtypeStruct((pairs, 1, lanes), jnp.float32),
        ),
        in_specs=[VMEM] * (2 + len(keys)),
        out_specs=(VMEM, VMEM),
        scratch_shapes=[pltpu.VMEM((span_rows, 2 * tokens), jnp.float32)],
        compiler_params=params(held + 4 * len(keys) * keys[0].size),
        cost_estimate=cost(
            2 * pairs * span_rows * lanes * HD, held, pairs * span_rows * lanes
        ),
    )(query_rot, bias, *keys)


def mix_kernel(n_chips, group, where, *refs):
    weight_refs, total_refs, refs = refs[:2], refs[2:4], refs[4:]
    value_refs, out_ref, buf, sems = refs[: 2 * n_chips], refs[-3], refs[-2], refs[-1]
    core = where[3]
    heads_here = value_refs[0].shape[1] // HD
    tokens = out_ref.shape[0]
    width = group * HD
    copies = []
    for side in range(2):
        first_head = (1 - core if side else core) * heads_here
        for i in range(heads_here):
            span = slice(i * HD, (i + 1) * HD)
            values = jnp.concatenate(
                [ref[:, span] for ref in value_refs[side * n_chips : (side + 1) * n_chips]],
                axis=0,
            )
            pair = side * heads_here + i
            mixed = jnp.dot(
                values.T, weight_refs[side][i], preferred_element_type=jnp.float32
            ) * (1.0 / total_refs[side][i])
            for g in range(group):
                buf[pair, :, g * HD : (g + 1) * HD] = mixed[
                    :, g * tokens : (g + 1) * tokens
                ].T.astype(jnp.bfloat16)
            start = pl.multiple_of((first_head + i) * width, width)
            copies.append(
                pltpu.make_async_copy(
                    buf.at[pair], out_ref.at[:, pl.ds(start, width)], sems.at[pair]
                )
            )
            copies[-1].start()
    for copy in copies:
        copy.wait()


def on_device(n_ctx, n_dp, x_tokens, queries, key_weight, value_weight, positions, block_lists):
    n_line, n_chips = n_dp // 2, n_ctx // 2
    tokens_local, query_local = x_tokens[0], queries[0]
    tok_rows, query_width = query_local.shape
    shard_rows, key_width = key_weight.shape
    half_rows, half_columns = shard_rows // 2, key_width // 2
    group = query_width // key_width
    ctx, dp = lax.axis_index("ctx"), lax.axis_index("dp")
    chip, core = ctx // 2, ctx % 2
    y = chip % 2
    where = jnp.stack([dp // 2, dp % 2, y, core, chip]).astype(jnp.int32)

    def over_core(array):
        return lax.ppermute(array, "ctx", [(i, i ^ 1) for i in range(n_ctx)])

    def over_y(array):
        return lax.ppermute(array, "ctx", [(i, i ^ 2) for i in range(n_ctx)])

    def over_x(array):
        return lax.ppermute(array, "dp", [(i, i ^ 1) for i in range(n_dp)])

    def over_z(array, step):
        return lax.ppermute(array, "dp", [(i, (i + 2 * step) % n_dp) for i in range(n_dp)])

    def over_xy(array):
        pairs = [
            (i * n_dp + d, (i ^ 2) * n_dp + (d ^ 1)) for i in range(n_ctx) for d in range(n_dp)
        ]
        return lax.ppermute(array, ("ctx", "dp"), pairs)

    def from_chip(array, step):
        return lax.ppermute(array, "ctx", [(i, (i + 2 * step) % n_ctx) for i in range(n_ctx)])

    def spread_out(arrays):
        return over_x(arrays[1]), over_y(arrays[2]), over_xy(arrays[3])

    up = n_line // 2

    def gather_pieces(own, late, after):
        came = [None] * n_line
        came[0] = own
        for j in range(1, up + 1):
            k = n_line - j
            if k > up:
                came[k] = over_z(came[(k + 1) % n_line], -1)
            before = came[j - 1]
            if j == up and (late or after):
                before = lax.optimization_barrier(
                    (before, *([came[up + 1]] if late else []), *after)
                )[0]
            came[j] = over_z(before, 1)
        return came

    key_own = cut_weight(where, key_weight)
    cuts = cut_tokens(where, tokens_local, n_line, key_own)
    key_pieces = gather_pieces(key_own, True, [])
    held = [cuts[0], over_x(cuts[1]), over_y(cuts[2]), over_xy(cuts[3])]
    value_own = cut_weight(where, value_weight, cuts[0])
    value_pieces = gather_pieces(value_own, False, [])

    positions = lax.optimization_barrier((positions, key_pieces[1]))[0]
    token_pos = positions[0]
    pos_pair = jnp.stack([token_pos, over_core(positions)[0]])
    pos_chip = jnp.where(core == 0, pos_pair, pos_pair[::-1]).reshape(-1)
    cosine, sine_part = rope_tables(pos_chip)
    own_rows = core * tok_rows
    query_cosine = lax.dynamic_slice_in_dim(cosine, own_rows, tok_rows, 0)
    query_sine = lax.dynamic_slice_in_dim(sine_part, own_rows, tok_rows, 0)
    n_heads = query_width // HD
    query_rot = pl.pallas_call(
        turn_queries_kernel,
        out_shape=jax.ShapeDtypeStruct((n_heads, tok_rows, HD), jnp.bfloat16),
        in_specs=[SMEM] + [VMEM] * 3 + [ANY],
        out_specs=VMEM,
        compiler_params=params(4 * query_local.size),
        cost_estimate=cost(3 * query_local.size, 4 * query_local.size),
    )(where, query_local, query_cosine, query_sine, key_pieces[1])

    chip_rows = 2 * tok_rows
    bias = pl.pallas_call(
        functools.partial(mask_kernel, chip_rows, n_chips),
        out_shape=jax.ShapeDtypeStruct((n_chips * chip_rows, tok_rows), jnp.bfloat16),
        in_specs=[SMEM, SMEM, ANY],
        out_specs=VMEM,
        compiler_params=params(16 * chip_rows * tok_rows),
        cost_estimate=cost(20 * n_chips * chip_rows * tok_rows, 0),
    )(where, block_lists[0], key_pieces[1])

    held[1:3] = lax.optimization_barrier((*held[1:3], key_pieces[up], value_pieces[1], query_rot, bias, cosine, sine_part))[:2]
    f32, bf16 = jnp.float32, jnp.bfloat16
    every = list(range(n_line))
    sets = [(array, over_core(array)) for array in held[:3]]
    key_x, key_y = project(where, sets[1:], every, key_pieces, None, (f32,), bias, cosine, sine_part)
    *held[3:], _ = lax.optimization_barrier((held[3], held[1], value_pieces[-1]))
    sets.append((held[3], over_core(held[3])))
    key_own_part, key_xy = project(
        where, [sets[0], sets[3]], every, key_pieces, None, (f32,), key_x
    )
    key_parts = (key_own_part, key_x, key_y, key_xy)
    key_here = pl.pallas_call(
        finish_keys_kernel,
        out_shape=jax.ShapeDtypeStruct(key_parts[0].shape, bf16),
        in_specs=[VMEM] * 6,
        out_specs=VMEM,
        compiler_params=params(26 * key_parts[0].size),
        cost_estimate=cost(6 * key_parts[0].size, 26 * key_parts[0].size),
    )(
        key_parts[0], *spread_out(key_parts), cosine, sine_part,
    )
    keys = [key_here] + [from_chip(key_here, j) for j in range(1, n_chips)]
    keys_other = [over_core(array) for array in keys]

    early = [j for j in every if j != up]
    early_values = project(where, sets, early, value_pieces, None, (f32,), key_parts[0])
    value_parts = project(where, sets, [up], value_pieces, early_values, (bf16,))
    value_here = pl.pallas_call(
        finish_values_kernel,
        out_shape=jax.ShapeDtypeStruct(value_parts[0].shape, bf16),
        in_specs=[VMEM] * 4,
        out_specs=VMEM,
        compiler_params=params(10 * value_parts[0].size),
        cost_estimate=cost(3 * value_parts[0].size, 10 * value_parts[0].size),
    )(value_parts[0], *spread_out(value_parts))
    weights, totals = weigh(query_rot, bias, keys, 0, group)
    values = [value_here] + [from_chip(value_here, j) for j in range(1, n_chips)]
    *values, weights = lax.optimization_barrier((*values, weights))
    values += [over_core(array) for array in values]
    weights_other, totals_other = weigh(query_rot, bias, keys_other, n_heads // 2, group)

    span_rows = n_chips * chip_rows
    pairs = n_heads // group
    held = 2 * tok_rows * (query_width + n_heads * span_rows)
    mixed = pl.pallas_call(
        functools.partial(mix_kernel, n_chips, group),
        out_shape=jax.ShapeDtypeStruct((tok_rows, query_width), bf16),
        in_specs=[SMEM] + [VMEM] * (4 + len(values)),
        out_specs=ANY,
        scratch_shapes=[
            pltpu.VMEM((pairs, tok_rows, group * HD), bf16),
            pltpu.SemaphoreType.DMA((pairs,)),
        ],
        compiler_params=params(held + 4 * span_rows * key_width),
        cost_estimate=cost(2 * tok_rows * query_width * span_rows, held),
    )(where, weights, weights_other, totals, totals_other, *values)
    return mixed[None]


def solution(mesh):
    return jax.shard_map(
        functools.partial(on_device, mesh.shape["ctx"], mesh.shape["dp"]),
        mesh=mesh,
        in_specs=(
            P("dp", "ctx", None),
            P("dp", "ctx", None),
            P("dp", None),
            P("dp", None),
            P("dp", "ctx"),
            P("dp", "ctx", None),
        ),
        out_specs=P("dp", "ctx", None),
        check_vma=False,
    )
```

```python
import functools
import math

import jax
import jax.numpy as jnp
from jax import lax
from jax.experimental import pallas as pl
from jax.experimental.pallas import tpu as pltpu
from jax.sharding import PartitionSpec as P

HD = 128
BLOCK = 64
LOG2E = 1.4426950408889634

neg_large = -1e30
HEADROOM = 2 * 1024 * 1024
ANY = pl.BlockSpec(memory_space=pl.ANY)
VMEM = pl.BlockSpec(memory_space=pltpu.VMEM)
SMEM = pl.BlockSpec(memory_space=pltpu.SMEM)


def params(held):
    return pltpu.CompilerParams(vmem_limit_bytes=held + HEADROOM)


def cost(flops, bytes_accessed, transcendentals=0):
    return pl.CostEstimate(
        flops=flops, bytes_accessed=bytes_accessed, transcendentals=transcendentals
    )


def rope_periods(half_width):
    return jnp.array(
        [
            int(2.0 * math.pi * 500000.0 ** (column / half_width) + 0.5)
            for column in range(half_width)
        ],
        jnp.int32,
    )


def rope_tables(token_pos):
    half_width = HD // 2
    periods = rope_periods(half_width)
    turn_counts = jnp.remainder(token_pos[:, None], periods[None, :])
    angles = 2.0 * math.pi * turn_counts.astype(jnp.float32) / periods.astype(jnp.float32)
    cosine = jnp.cos(angles)
    sine_part = jnp.sin(angles)
    return (
        jnp.concatenate([cosine, cosine], axis=1),
        jnp.concatenate([-sine_part, sine_part], axis=1),
    )


def turn(head, cosine, sine_part):
    return head * cosine + pltpu.roll(head, HD // 2, 1) * sine_part


def part_of(weight_ref, where, shape):
    rows, columns = shape
    y, core = where[2], where[3]
    return weight_ref[
        pl.ds(pl.multiple_of(y * rows, rows), rows),
        pl.ds(pl.multiple_of(core * columns, columns), columns),
    ]


def cut_weight_kernel(where, weight_ref, *refs):
    refs[-1][...] = part_of(weight_ref, where, refs[-1].shape)


def cut_weight(where, weight, *after):
    part = (weight.shape[0] // 2, weight.shape[1] // 2)
    return pl.pallas_call(
        cut_weight_kernel,
        out_shape=jax.ShapeDtypeStruct(part, jnp.bfloat16),
        in_specs=[SMEM, VMEM] + [ANY] * len(after),
        out_specs=VMEM,
        compiler_params=params(4 * weight.size),
        cost_estimate=cost(0, 3 * weight.size),
    )(where, weight, *after)


def cut_tokens_kernel(n_line, where, x_ref, *refs):
    out_refs = refs[-4:]
    z, x, y = where[0], where[1], where[2]
    width = out_refs[0].shape[2]
    for i in (1, 2, 3, 0):
        for j in range(n_line):
            shard = lax.rem(z - j + n_line, n_line) * 2 + (1 - x if i & 1 else x)
            half = 1 - y if i & 2 else y
            start = pl.multiple_of((shard * 2 + half) * width, width)
            out_refs[i][j] = x_ref[:, pl.ds(start, width)]


def cut_tokens(where, tokens, n_line, *after):
    rows, columns = tokens.shape
    shape = (n_line, rows, columns // (4 * n_line))
    return pl.pallas_call(
        functools.partial(cut_tokens_kernel, n_line),
        out_shape=(jax.ShapeDtypeStruct(shape, jnp.bfloat16),) * 4,
        in_specs=[SMEM, VMEM] + [ANY] * len(after),
        out_specs=(VMEM,) * 4,
        compiler_params=pltpu.CompilerParams(vmem_limit_bytes=52 * 1024 * 1024),
        cost_estimate=cost(0, 4 * tokens.size),
    )(where, tokens, *after)


def project_kernel(n_sets, lines, with_start, n_after, where, *refs):
    n_parts = len(lines)
    refs = list(refs)
    x_refs, refs = refs[: 2 * n_sets], refs[2 * n_sets :]
    w_refs, refs = refs[:n_parts], refs[n_parts:]
    start_refs, refs = (refs[:n_sets], refs[n_sets:]) if with_start else (None, refs)
    outs = refs[n_after:]
    core = where[3]
    tokens = x_refs[0].shape[1]
    for s in range(n_sets):
        for side in range(2):
            x_ref = x_refs[2 * s + side]
            place = pl.ds(pl.multiple_of((1 - core if side else core) * tokens, tokens), tokens)
            total = start_refs[s][place, :] if with_start else None
            for j, w_ref in zip(lines, w_refs):
                term = jnp.dot(x_ref[j], w_ref[...], preferred_element_type=jnp.float32)
                total = term if total is None else total + term
            for out in outs[s::n_sets]:
                out[place, :] = total.astype(out.dtype)


def project(where, sets, lines, pieces, starts, out_types, *after):
    n_line, tokens, rows = sets[0][0].shape
    columns = pieces[0].shape[1]
    n_parts, n_sets = len(lines), len(sets)
    pieces = [pieces[j] for j in lines]
    x_args = [array for pair in sets for array in pair]
    starts = list(starts or [])
    shapes = tuple(
        jax.ShapeDtypeStruct((2 * tokens, columns), t) for t in out_types for _ in sets
    )
    held = n_sets * 4 * tokens * (n_line * rows + 4 * columns) + 2 * n_parts * rows * columns
    return pl.pallas_call(
        functools.partial(project_kernel, n_sets, lines, bool(starts), len(after)),
        out_shape=shapes,
        in_specs=[SMEM]
        + [VMEM] * len(x_args)
        + [VMEM] * (n_parts + len(starts))
        + [ANY] * len(after),
        out_specs=(VMEM,) * len(shapes),
        compiler_params=params(held),
        cost_estimate=cost(4 * n_sets * tokens * n_parts * rows * columns, held),
    )(where, *x_args, *pieces, *starts, *after)


def add_up(refs, span=slice(None)):
    total = refs[0][:, span].astype(jnp.float32)
    for ref in refs[1:]:
        total = total + ref[:, span].astype(jnp.float32)
    return total


def finish_keys_kernel(own_ref, x_ref, y_ref, xy_ref, cosine_ref, sine_ref, out_ref):
    for h in range(out_ref.shape[1] // HD):
        span = slice(h * HD, (h + 1) * HD)
        key = add_up((own_ref, x_ref, y_ref, xy_ref), span)
        out_ref[:, span] = turn(key, cosine_ref[...], sine_ref[...]).astype(jnp.bfloat16)


def finish_values_kernel(own_ref, x_ref, y_ref, xy_ref, out_ref):
    out_ref[...] = add_up((own_ref, x_ref, y_ref, xy_ref)).astype(jnp.bfloat16)


def turn_queries_kernel(where, q_ref, cosine_ref, sine_ref, after_ref, out_ref):
    half = out_ref.shape[0] // 2
    core = where[3]
    for h in range(2 * half):
        side = 1 - core if h // half else core
        start = pl.multiple_of((side * half + h % half) * HD, HD)
        query = q_ref[:, pl.ds(start, HD)].astype(jnp.float32)
        out_ref[h] = turn(query, cosine_ref[...], sine_ref[...]).astype(jnp.bfloat16)


def mask_kernel(chip_rows, n_chips, where, lists_ref, *refs):
    out_ref = refs[-1]
    tokens = out_ref.shape[1]
    chip, core = where[4], where[3]
    shape = (BLOCK, tokens)
    row, column = (lax.broadcasted_iota(jnp.int32, shape, axis) for axis in range(2))
    ahead = row - column
    first_query = chip * chip_rows + core * tokens
    for j in range(n_chips):
        for b in range(chip_rows // BLOCK):
            first_key = lax.rem(chip - j + n_chips, n_chips) * chip_rows + b * BLOCK
            listed = ahead > tokens + BLOCK
            for q in range(lists_ref.shape[0]):
                found = lists_ref[q, 0] == first_key // BLOCK
                for entry in range(1, lists_ref.shape[1]):
                    found = found | (lists_ref[q, entry] == first_key // BLOCK)
                limit = jnp.where(found, first_query - first_key, -tokens - BLOCK)
                listed = listed | ((column // BLOCK == q) & (ahead <= limit))
            rows = slice(j * chip_rows + b * BLOCK, j * chip_rows + (b + 1) * BLOCK)
            out_ref[rows, :] = jnp.where(listed, 0.0, neg_large).astype(jnp.bfloat16)


def weigh_kernel(first, group, q_ref, bias_ref, *refs):
    key_refs, (weight_ref, total_ref, scores) = refs[:-3], refs[-3:]
    tokens = q_ref.shape[1]
    span_rows, lanes = scores.shape
    together = lanes // tokens
    scale = HD ** (-0.5) * LOG2E
    square = (tokens, tokens)
    row, column = (lax.broadcasted_iota(jnp.int32, square, axis) for axis in range(2))
    pick = (row == column).astype(jnp.float32).astype(jnp.bfloat16)
    for pair in range(weight_ref.shape[0]):
        span = slice(pair * HD, (pair + 1) * HD)
        keys = jnp.concatenate([ref[:, span] for ref in key_refs], axis=0)
        keys = jnp.concatenate([keys, bias_ref[...]], axis=1)
        for g in range(0, group, together):
            head = first + pair * group + g
            query = jnp.concatenate(
                [jnp.concatenate([q_ref[head + t], pick], axis=1) for t in range(together)],
                axis=0,
            )
            scores[...] = lax.dot_general(
                keys, query, (((1,), (1,)), ((), ())), preferred_element_type=jnp.float32
            )
            top = scores[:8]
            for r in range(8, span_rows, 8):
                top = jnp.maximum(top, scores[r : r + 8])
            top = jnp.max(top, axis=0, keepdims=True)
            total = jnp.zeros((16, lanes), jnp.float32)
            columns = slice(g * tokens, g * tokens + lanes)
            for r in range(0, span_rows, 16):
                probabilities = jnp.exp2((scores[r : r + 16] - top) * scale)
                total = total + probabilities
                weight_ref[pair, r : r + 16, columns] = probabilities.astype(jnp.bfloat16)
            total_ref[pair, :, columns] = jnp.sum(total, axis=0, keepdims=True)


def weigh(query_rot, bias, keys, first, group):
    _, tokens, _ = query_rot.shape
    span_rows = bias.shape[0]
    pairs, lanes = keys[0].shape[1] // HD, group * tokens
    held = 2 * query_rot.size + 10 * bias.size + 2 * pairs * span_rows * lanes
    return pl.pallas_call(
        functools.partial(weigh_kernel, first, group),
        out_shape=(
            jax.ShapeDtypeStruct((pairs, span_rows, lanes), jnp.bfloat16),
            jax.ShapeDtypeStruct((pairs, 1, lanes), jnp.float32),
        ),
        in_specs=[VMEM] * (2 + len(keys)),
        out_specs=(VMEM, VMEM),
        scratch_shapes=[pltpu.VMEM((span_rows, 2 * tokens), jnp.float32)],
        compiler_params=params(held + 4 * len(keys) * keys[0].size),
        cost_estimate=cost(
            2 * pairs * span_rows * lanes * HD, held, pairs * span_rows * lanes
        ),
    )(query_rot, bias, *keys)


def mix_kernel(n_chips, group, where, *refs):
    weight_refs, total_refs, refs = refs[:2], refs[2:4], refs[4:]
    value_refs, out_ref, buf, sems = refs[: 2 * n_chips], refs[-3], refs[-2], refs[-1]
    core = where[3]
    heads_here = value_refs[0].shape[1] // HD
    tokens = out_ref.shape[0]
    width = group * HD
    copies = []
    for side in range(2):
        first_head = (1 - core if side else core) * heads_here
        for i in range(heads_here):
            span = slice(i * HD, (i + 1) * HD)
            values = jnp.concatenate(
                [ref[:, span] for ref in value_refs[side * n_chips : (side + 1) * n_chips]],
                axis=0,
            )
            pair = side * heads_here + i
            columns = values.T
            step = group // 2
            for g in range(0, group, step):
                lanes = slice(g * tokens, (g + step) * tokens)
                mixed = jnp.dot(
                    columns, weight_refs[side][i, :, lanes], preferred_element_type=jnp.float32
                ) * (1.0 / total_refs[side][i, :, lanes])
                for t in range(step):
                    buf[pair, :, (g + t) * HD : (g + t + 1) * HD] = mixed[
                        :, t * tokens : (t + 1) * tokens
                    ].T.astype(jnp.bfloat16)
                start = pl.multiple_of((first_head + i) * width + g * HD, step * HD)
                copies.append(
                    pltpu.make_async_copy(
                        buf.at[pair, :, pl.ds(g * HD, step * HD)],
                        out_ref.at[:, pl.ds(start, step * HD)],
                        sems.at[pair, g // step],
                    )
                )
                copies[-1].start()
    for copy in copies:
        copy.wait()


def on_device(n_ctx, n_dp, x_tokens, queries, key_weight, value_weight, positions, block_lists):
    n_line, n_chips = n_dp // 2, n_ctx // 2
    tokens_local, query_local = x_tokens[0], queries[0]
    tok_rows, query_width = query_local.shape
    shard_rows, key_width = key_weight.shape
    half_rows, half_columns = shard_rows // 2, key_width // 2
    group = query_width // key_width
    ctx, dp = lax.axis_index("ctx"), lax.axis_index("dp")
    chip, core = ctx // 2, ctx % 2
    y = chip % 2
    where = jnp.stack([dp // 2, dp % 2, y, core, chip]).astype(jnp.int32)

    def over_core(array):
        return lax.ppermute(array, "ctx", [(i, i ^ 1) for i in range(n_ctx)])

    def over_y(array):
        return lax.ppermute(array, "ctx", [(i, i ^ 2) for i in range(n_ctx)])

    def over_x(array):
        return lax.ppermute(array, "dp", [(i, i ^ 1) for i in range(n_dp)])

    def over_z(array, step):
        return lax.ppermute(array, "dp", [(i, (i + 2 * step) % n_dp) for i in range(n_dp)])

    def over_xy(array):
        pairs = [
            (i * n_dp + d, (i ^ 2) * n_dp + (d ^ 1)) for i in range(n_ctx) for d in range(n_dp)
        ]
        return lax.ppermute(array, ("ctx", "dp"), pairs)

    def from_chip(array, step):
        return lax.ppermute(array, "ctx", [(i, (i + 2 * step) % n_ctx) for i in range(n_ctx)])

    def spread_out(arrays):
        came_y, came_xy = over_y(arrays[2]), over_xy(arrays[3])
        return over_x(arrays[1]), came_y, came_xy

    up = n_line // 2

    def gather_pieces(own, late, after):
        came = [None] * n_line
        came[0] = own
        for j in range(1, up + 1):
            k = n_line - j
            if k > up:
                came[k] = over_z(came[(k + 1) % n_line], -1)
            before = came[j - 1]
            if j == up and (late or after):
                before = lax.optimization_barrier(
                    (before, *([came[up + 1]] if late else []), *after)
                )[0]
            came[j] = over_z(before, 1)
        return came

    key_own = cut_weight(where, key_weight)
    cuts = cut_tokens(where, tokens_local, n_line, key_own)
    key_pieces = gather_pieces(key_own, True, [])
    held = [cuts[0], over_x(cuts[1]), over_y(cuts[2]), over_xy(cuts[3])]
    value_own = cut_weight(where, value_weight, cuts[0])
    value_pieces = gather_pieces(value_own, False, [])

    positions = lax.optimization_barrier((positions, key_pieces[1]))[0]
    token_pos = positions[0]
    pos_pair = jnp.stack([token_pos, over_core(positions)[0]])
    pos_chip = jnp.where(core == 0, pos_pair, pos_pair[::-1]).reshape(-1)
    cosine, sine_part = rope_tables(pos_chip)
    own_rows = core * tok_rows
    query_cosine = lax.dynamic_slice_in_dim(cosine, own_rows, tok_rows, 0)
    query_sine = lax.dynamic_slice_in_dim(sine_part, own_rows, tok_rows, 0)
    n_heads = query_width // HD
    query_rot = pl.pallas_call(
        turn_queries_kernel,
        out_shape=jax.ShapeDtypeStruct((n_heads, tok_rows, HD), jnp.bfloat16),
        in_specs=[SMEM] + [VMEM] * 3 + [ANY],
        out_specs=VMEM,
        compiler_params=params(4 * query_local.size),
        cost_estimate=cost(3 * query_local.size, 4 * query_local.size),
    )(where, query_local, query_cosine, query_sine, key_pieces[1])

    chip_rows = 2 * tok_rows
    bias = pl.pallas_call(
        functools.partial(mask_kernel, chip_rows, n_chips),
        out_shape=jax.ShapeDtypeStruct((n_chips * chip_rows, tok_rows), jnp.bfloat16),
        in_specs=[SMEM, SMEM, ANY],
        out_specs=VMEM,
        compiler_params=params(16 * chip_rows * tok_rows),
        cost_estimate=cost(20 * n_chips * chip_rows * tok_rows, 0),
    )(where, block_lists[0], key_pieces[1])

    held[1:3] = lax.optimization_barrier((*held[1:3], key_pieces[up], value_pieces[1], query_rot, bias, cosine, sine_part))[:2]
    f32, bf16 = jnp.float32, jnp.bfloat16
    every = list(range(n_line))
    sets = [(array, over_core(array)) for array in held[:3]]
    (key_y,) = project(where, sets[2:], every, key_pieces, None, (f32,), bias, cosine, sine_part)
    (key_x,) = project(where, sets[1:2], every, key_pieces, None, (f32,), key_y)
    *held[3:], _ = lax.optimization_barrier((held[3], held[1], value_pieces[-1]))
    sets.append((held[3], over_core(held[3])))
    key_own_part, key_xy = project(
        where, [sets[0], sets[3]], every, key_pieces, None, (f32,), key_x
    )
    key_parts = (key_own_part, key_x, key_y, key_xy)
    key_here = pl.pallas_call(
        finish_keys_kernel,
        out_shape=jax.ShapeDtypeStruct(key_parts[0].shape, bf16),
        in_specs=[VMEM] * 6,
        out_specs=VMEM,
        compiler_params=params(26 * key_parts[0].size),
        cost_estimate=cost(6 * key_parts[0].size, 26 * key_parts[0].size),
    )(
        key_parts[0], *spread_out(key_parts), cosine, sine_part,
    )
    keys = [key_here] + [from_chip(key_here, j) for j in range(1, n_chips)]
    keys_other = [over_core(array) for array in keys]

    early = [j for j in every if j != up]
    early_values = project(where, sets, early, value_pieces, None, (f32,), key_parts[0])
    value_parts = project(where, sets, [up], value_pieces, early_values, (bf16,))
    value_here = pl.pallas_call(
        finish_values_kernel,
        out_shape=jax.ShapeDtypeStruct(value_parts[0].shape, bf16),
        in_specs=[VMEM] * 4,
        out_specs=VMEM,
        compiler_params=params(10 * value_parts[0].size),
        cost_estimate=cost(3 * value_parts[0].size, 10 * value_parts[0].size),
    )(value_parts[0], *spread_out(value_parts))
    weights, totals = weigh(query_rot, bias, keys, 0, group)
    values = [value_here] + [from_chip(value_here, j) for j in range(1, n_chips)]
    *values, weights = lax.optimization_barrier((*values, weights))
    values += [over_core(array) for array in values]
    weights_other, totals_other = weigh(query_rot, bias, keys_other, n_heads // 2, group)

    span_rows = n_chips * chip_rows
    pairs = n_heads // group
    held = 2 * tok_rows * (query_width + n_heads * span_rows)
    mixed = pl.pallas_call(
        functools.partial(mix_kernel, n_chips, group),
        out_shape=jax.ShapeDtypeStruct((tok_rows, query_width), bf16),
        in_specs=[SMEM] + [VMEM] * (4 + len(values)),
        out_specs=ANY,
        scratch_shapes=[
            pltpu.VMEM((pairs, tok_rows, group * HD), bf16),
            pltpu.SemaphoreType.DMA((pairs, 2)),
        ],
        compiler_params=params(held + 4 * span_rows * key_width),
        cost_estimate=cost(2 * tok_rows * query_width * span_rows, held),
    )(where, weights, weights_other, totals, totals_other, *values)
    return mixed[None]


def solution(mesh):
    return jax.shard_map(
        functools.partial(on_device, mesh.shape["ctx"], mesh.shape["dp"]),
        mesh=mesh,
        in_specs=(
            P("dp", "ctx", None),
            P("dp", "ctx", None),
            P("dp", None),
            P("dp", None),
            P("dp", "ctx"),
            P("dp", "ctx", None),
        ),
        out_specs=P("dp", "ctx", None),
        check_vma=False,
    )
```
